32 devices in a mesh: query: 4 (over y, x), context: 8 (over z, core).
Axes of the slice: x: 2, y: 2, z: 4, core: 2. Of those that a mesh axis runs over, the one named last changes fastest.
Arguments:
- queries: bfloat16 [4, 1024, 128], P('query', 'context'), may hold values from -6 to 6
- keys: bfloat16 [1024, 128], P('context'), may hold values from -6 to 6
- values: bfloat16 [1024, 128], P('context'), may hold values from -6 to 6
- out_grad: bfloat16 [4, 1024, 128], P('query', 'context'), may hold values from -6 to 6
- prefix_states: bfloat16 [8, 8256, 128], P('context'), may hold values from -48 to 48
Outputs:
- grad_queries: bfloat16 [4, 1024, 128], P('query', 'context')
- grad_keys: bfloat16 [8, 128, 128], P('context', 'query')
- grad_values: bfloat16 [8, 128, 128], P('context', 'query')
The draws below stay inside these ranges and needn't reach their ends.
All inputs are finite; a program needn't handle non-finite values.
Results may differ from the reference program's by a relative error of at most 0.014.
Values may be sent and summed in bfloat16 or wider, within the bound.
A program may use at most 192 MiB of HBM per device.

```python
import jax
import jax.numpy as jnp
import numpy as np
from jax import lax

D = 128
TOK_DEV = 128
FEATURES = 8256
HEADS = 4
BLOCKS = 8
TOKENS = 1024


def level_of(rng, shape, shards, smallest, top_value):
    factor_of, own = 1.0, jax.random.fold_in(rng, 6)
    for axis_at, parts in shards:
        steps = jnp.exp(jax.random.uniform(jax.random.fold_in(own, axis_at), (parts,), jnp.float32, smallest / len(shards), top_value / len(shards)))
        factor_of = factor_of * jnp.repeat(steps, shape[axis_at] // parts).reshape([-1 if axis == axis_at else 1 for axis in range(len(shape))])
    return factor_of


def centred(rng, shape, spread, bound, shards=(), held_as=jnp.bfloat16):
    array = spread * jax.random.normal(rng, shape, jnp.float32)
    if shards:
        array = array * level_of(rng, shape, shards, -0.22, 0.18)
    return jnp.clip(array, -bound, bound).astype(held_as)


def setup_inputs(seed: int = 0) -> dict:
    key_of = jax.random.split(jax.random.key(seed), 6)
    queries = centred(key_of[0], (HEADS, TOKENS, D), 1.0, 6.0, ((0, 4), (1, 8)))
    keys = centred(key_of[1], (TOKENS, D), 1.0, 6.0, ((0, 8),))
    values = centred(key_of[2], (TOKENS, D), 1.0, 6.0, ((0, 8),))
    out_grad = centred(key_of[3], (HEADS, TOKENS, D), 1.0, 6.0, ((0, 4), (1, 8)))
    prefix_states = centred(key_of[4], (BLOCKS, FEATURES, D), (TOK_DEV // 16), 48.0, ((0, 8),))
    return {"queries": queries, "keys": keys, "values": values, "out_grad": out_grad, "prefix_states": prefix_states}


def pair_tables(model_width):
    first_index, second_index = np.triu_indices(model_width)
    pair_weight = np.where(first_index == second_index, 1.0, np.sqrt(2.0)).astype(np.float32)
    return (first_index.astype(np.int32), second_index.astype(np.int32), pair_weight)

def expand_rows(rows_in, first_index, second_index, pair_weight):
    column_form = rows_in.astype(jnp.float32).T
    return (column_form[first_index] * column_form[second_index] * pair_weight[:, None]).astype(jnp.bfloat16)

def pair_grad(feature_grad, column_form, first_index, second_index, pair_weight, onehot_first, onehot_second):
    weighted = feature_grad.astype(jnp.float32) * pair_weight[:, None]
    term_one = (weighted * column_form[second_index]).astype(jnp.bfloat16)
    term_two = (weighted * column_form[first_index]).astype(jnp.bfloat16)
    dims = (((0,), (0,)), ((), ()))
    return lax.dot_general(term_one, onehot_first, dims, preferred_element_type=jnp.float32) + lax.dot_general(term_two, onehot_second, dims, preferred_element_type=jnp.float32)

def reference(queries, keys, values, out_grad, prefix_states):
    head_count, token_count, model_width = queries.shape
    block_count = prefix_states.shape[0]
    row_count = token_count // block_count
    score_scale = 1.0 / (model_width * row_count)
    first_index, second_index, pair_weight = pair_tables(model_width)
    width_range = jnp.arange(model_width, dtype=jnp.int32)
    onehot_first = (jnp.asarray(first_index)[:, None] == width_range[None, :]).astype(jnp.bfloat16)
    onehot_second = (jnp.asarray(second_index)[:, None] == width_range[None, :]).astype(jnp.bfloat16)
    query_blocks = queries.reshape(head_count, block_count, row_count, model_width)
    grad_blocks = out_grad.reshape(head_count, block_count, row_count, model_width)
    key_blocks = keys.reshape(block_count, row_count, model_width)
    value_blocks = values.reshape(block_count, row_count, model_width)

    def block_state(index):
        total = jnp.zeros((first_index.shape[0], model_width), jnp.float32)
        for head_index in range(head_count):
            expanded = expand_rows(query_blocks[head_index, index], first_index, second_index, pair_weight)
            total = total + jnp.dot(expanded, grad_blocks[head_index, index], preferred_element_type=jnp.float32)
        return score_scale * total
    states = lax.map(block_state, jnp.arange(block_count, dtype=jnp.int32))
    later = jnp.cumsum(states[::-1], axis=0)[::-1]
    suffix = jnp.concatenate([later[1:], jnp.zeros_like(later[:1])], axis=0)
    causal = jnp.arange(row_count)[None, :] <= jnp.arange(row_count)[:, None]

    def block_grads(index):
        key_rows = key_blocks[index]
        value_rows = value_blocks[index]
        grad_state = suffix[index].astype(jnp.bfloat16)
        prefix = prefix_states[index]
        key_cols = key_rows.astype(jnp.float32).T
        expanded_keys = expand_rows(key_rows, first_index, second_index, pair_weight)
        value_sum = jnp.dot(expanded_keys.T, grad_state, preferred_element_type=jnp.float32)
        key_feature = jnp.dot(grad_state, value_rows.T, preferred_element_type=jnp.float32).astype(jnp.bfloat16)
        key_sum = pair_grad(key_feature, key_cols, first_index, second_index, pair_weight, onehot_first, onehot_second)
        query_list = []
        for head_index in range(head_count):
            query_rows = query_blocks[head_index, index]
            grad_rows = grad_blocks[head_index, index]
            score_dot = jnp.dot(query_rows, key_rows.T, preferred_element_type=jnp.float32)
            grad_dot = jnp.dot(grad_rows, value_rows.T, preferred_element_type=jnp.float32)
            attn = jnp.where(causal, score_scale * score_dot * score_dot, 0.0).astype(jnp.bfloat16)
            slope = jnp.where(causal, 2.0 * score_scale * score_dot * grad_dot, 0.0).astype(jnp.bfloat16)
            local_query = jnp.dot(slope, key_rows, preferred_element_type=jnp.float32)
            key_sum = key_sum + jnp.dot(slope.T, query_rows, preferred_element_type=jnp.float32)
            value_sum = value_sum + jnp.dot(attn.T, grad_rows, preferred_element_type=jnp.float32)
            query_feature = jnp.dot(prefix, grad_rows.T, preferred_element_type=jnp.float32).astype(jnp.bfloat16)
            cross_query = score_scale * pair_grad(query_feature, query_rows.astype(jnp.float32).T, first_index, second_index, pair_weight, onehot_first, onehot_second)
            query_list.append((local_query + cross_query).astype(jnp.bfloat16))
        return (jnp.stack(query_list), key_sum.astype(jnp.bfloat16), value_sum.astype(jnp.bfloat16))
    grad_q, grad_k, grad_v = lax.map(block_grads, jnp.arange(block_count, dtype=jnp.int32))
    grad_q = grad_q.transpose(1, 0, 2, 3).reshape(head_count, token_count, model_width)
    return (grad_q, grad_k, grad_v)
```

```python
import functools

import jax
import jax.numpy as jnp
import numpy as np
from jax import lax
from jax.experimental import pallas as pl
from jax.experimental.pallas import tpu as pltpu
from jax.sharding import PartitionSpec as P

MESH = pl.DeviceIdType.MESH
NT = (((1,), (1,)), ((), ()))
NN = (((1,), (0,)), ((), ()))


def dot(a, b, dims):
    return lax.dot_general(a, b, dims, preferred_element_type=jnp.float32)


def chunk_count(features, most=12):
    for count in range(most, 0, -1):
        if features % (16 * count) == 0:
            return count
    return 1


def kernel(
    q_ref, k_ref, v_ref, g_ref, p_ref, dq_ref, dk_ref, dv_ref,
    kk, vv, qb, gb, pb, fb, xt, red, acc, sb, rb,
    local_sem, p_sem, kv_send, kv_recv, z_send, z_recv, x_send, x_recv,
):
    heads = lax.axis_size("query")
    chips = lax.axis_size("context") // 2
    group = 2 * heads
    h = lax.axis_index("query")
    place = lax.axis_index("context")
    z, core = place // 2, place % 2
    me = core * heads + h
    rows, width = q_ref.shape[1], q_ref.shape[2]
    features = p_ref.shape[1]
    scale = 1.0 / (width * rows)
    share = rows // heads
    chunks = chunk_count(features)
    chunk = features // chunks

    loads = [
        pltpu.make_async_copy(q_ref.at[0], qb.at[0], local_sem.at[0]),
        pltpu.make_async_copy(g_ref.at[0], gb.at[0], local_sem.at[1]),
        pltpu.make_async_copy(k_ref, kk.at[core], local_sem.at[2]),
        pltpu.make_async_copy(v_ref, vv.at[core], local_sem.at[3]),
    ]
    for load in loads:
        load.start()
    p_loads = []
    for n in range(chunks):
        part = pl.ds(n * chunk, chunk)
        load = pltpu.make_async_copy(p_ref.at[0, part], pb.at[part], p_sem.at[n])
        load.start()
        p_loads.append(load)

    barrier = pltpu.get_barrier_semaphore()

    def peer(offset):
        other = lax.rem(me + offset, group)
        return {"query": other % heads, "context": 2 * z + other // heads}

    for offset in range(1, group):
        pl.semaphore_signal(barrier, inc=1, device_id=peer(offset), device_id_type=MESH)
    for step in range(1, chips):
        @pl.when(z + step < chips)
        def _():
            pl.semaphore_signal(
                barrier, inc=1, device_id={"context": place + 2 * step}, device_id_type=MESH
            )
    pl.semaphore_wait(barrier, group - 1 + z)

    def down(step):
        return [
            pltpu.make_async_remote_copy(
                src_ref=src.at[0],
                dst_ref=dst.at[step],
                send_sem=z_send.at[which, step],
                recv_sem=z_recv.at[which, step],
                device_id={"context": place - 2 * step},
                device_id_type=MESH,
            )
            for which, (src, dst) in enumerate(((q_ref, qb), (g_ref, gb)))
        ]

    for step in range(chips - 1, 0, -1):
        @pl.when(z >= step)
        def _():
            for copy in down(step):
                copy.start()

    kv = [
        pltpu.make_async_remote_copy(
            src_ref=src,
            dst_ref=dst.at[core],
            send_sem=kv_send.at[which],
            recv_sem=kv_recv.at[which],
            device_id={"context": place + 1 - 2 * core},
            device_id_type=MESH,
        )
        for which, (src, dst) in enumerate(((k_ref, kk), (v_ref, vv)))
    ]
    for copy in kv:
        copy.start()
    for load in loads:
        load.wait()

    q_own, g_own = qb[0], gb[0]
    xt[...] = q_own.astype(jnp.float32).T
    zero = h // heads
    spot = lax.broadcasted_iota(jnp.int32, (8, rows), 0)
    done, filled = 0, 0
    total = jnp.zeros((width, rows), jnp.float32)
    cross = []
    for tile in range(width // 8):
        length = width - 8 * tile
        last = 8 * tile + 8
        need = last * width - last * (last - 1) // 2
        while filled < need:
            p_loads[done].wait()
            part = pl.ds(filled, chunk)
            fb[part, :] = dot(pb[part, :], g_own, NT)
            done, filled = done + 1, filled + chunk
        x_tile = xt[8 * tile:, :]

        def one(r, total, tile=tile, length=length, x_tile=x_tile):
            i = 8 * tile + r
            begin = i * width - (i * (i - 1)) // 2 - r + zero
            feat = fb[pl.ds(begin, length), :]
            weight = jnp.where(spot < r, 0.0, jnp.where(spot == r, np.float32(np.sqrt(0.5)), 1.0))
            head = feat[:8] * weight
            feat = jnp.concatenate([head, feat[8:]], axis=0) if length > 8 else head
            row = xt[pl.ds(i + zero, 1), :]
            red[i] = jnp.sum((feat * x_tile).reshape(length // 8, 8, rows), axis=0)
            return total + feat * row

        total = lax.fori_loop(0, 8, one, total, unroll=8)
        cross.append(total[:8])
        total = total[8:]
    cross_t = jnp.concatenate(cross, axis=0) + jnp.sum(red[...], axis=1)
    cross_q = (scale * np.sqrt(2.0)) * cross_t.T

    for copy in kv:
        copy.wait()
    keys = kk[...].reshape(2 * rows, width)
    vals = vv[...].reshape(2 * rows, width)

    def weights(q, g):
        score = dot(keys, q, NT)
        return scale * score * score, (2.0 * scale) * score * dot(vals, g, NT)

    attn, slope = weights(q_own, g_own)
    key_at = lax.broadcasted_iota(jnp.int32, (2 * rows, rows), 0)
    query_at = lax.broadcasted_iota(jnp.int32, (2 * rows, rows), 1) + core * rows
    causal = key_at <= query_at
    attn = jnp.where(causal, attn, 0.0).astype(jnp.bfloat16)
    slope = jnp.where(causal, slope, 0.0).astype(jnp.bfloat16)
    acc[:, :width] = dot(slope, q_own, NN)
    acc[:, width:] = dot(attn, g_own, NN)
    own_score = dot(q_own, kk[core], NT)
    own_slope = (2.0 * scale) * own_score * dot(g_own, vv[core], NT)
    own_causal = lax.broadcasted_iota(jnp.int32, (rows, rows), 1) <= lax.broadcasted_iota(
        jnp.int32, (rows, rows), 0
    )
    own_slope = jnp.where(own_causal, own_slope, 0.0).astype(jnp.bfloat16)
    dq_ref[0] = (dot(own_slope, kk[core], NN) + cross_q).astype(dq_ref.dtype)

    for step in range(1, chips):
        @pl.when(z + step < chips)
        def _():
            for copy in down(step):
                copy.wait_recv()
            q, g = qb[step], gb[step]
            attn, slope = weights(q, g)
            acc[:, :width] += dot(slope.astype(jnp.bfloat16), q, NN)
            acc[:, width:] += dot(attn.astype(jnp.bfloat16), g, NN)

    sb[...] = acc[...].astype(jnp.bfloat16).reshape(group, share, 2 * width)
    swaps = []
    for offset in range(1, group):
        other = lax.rem(me + offset, group)
        copy = pltpu.make_async_remote_copy(
            src_ref=sb.at[other],
            dst_ref=rb.at[offset],
            send_sem=x_send.at[offset],
            recv_sem=x_recv.at[offset],
            device_id=peer(offset),
            device_id_type=MESH,
        )
        copy.start()
        swaps.append(copy)
    mine = acc[pl.ds(pl.multiple_of(me * share, share), share), :]
    for offset, copy in enumerate(swaps, 1):
        copy.wait_recv()
        mine = mine + rb[offset].astype(jnp.float32)
    dk_ref[0] = mine[:, :width].astype(dk_ref.dtype)
    dv_ref[0] = mine[:, width:].astype(dv_ref.dtype)

    for copy in swaps:
        copy.wait_send()
    for step in range(1, chips):
        @pl.when(z >= step)
        def _():
            for copy in down(step):
                copy.wait_send()


def body(queries, keys, values, out_grad, prefix_states):
    heads = lax.axis_size("query")
    chips = lax.axis_size("context") // 2
    group = 2 * heads
    rows, width = keys.shape
    features = prefix_states.shape[1]
    share = rows // heads
    chunks = chunk_count(features)
    half = jax.ShapeDtypeStruct((1, share, width), jnp.bfloat16)
    dma = pltpu.SemaphoreType.DMA
    return pl.pallas_call(
        kernel,
        out_shape=(jax.ShapeDtypeStruct(queries.shape, jnp.bfloat16), half, half),
        in_specs=[pl.BlockSpec(memory_space=pl.ANY)] * 5,
        out_specs=[pl.BlockSpec(memory_space=pltpu.VMEM)] * 3,
        scratch_shapes=[
            pltpu.VMEM((2, rows, width), jnp.bfloat16),
            pltpu.VMEM((2, rows, width), jnp.bfloat16),
            pltpu.VMEM((chips, rows, width), jnp.bfloat16),
            pltpu.VMEM((chips, rows, width), jnp.bfloat16),
            pltpu.VMEM((features, width), jnp.bfloat16),
            pltpu.VMEM((features, rows), jnp.float32),
            pltpu.VMEM((width, rows), jnp.float32),
            pltpu.VMEM((width, 8, rows), jnp.float32),
            pltpu.VMEM((2 * rows, 2 * width), jnp.float32),
            pltpu.VMEM((group, share, 2 * width), jnp.bfloat16),
            pltpu.VMEM((group, share, 2 * width), jnp.bfloat16),
            dma((4,)),
            dma((chunks,)),
            dma((2,)),
            dma((2,)),
            dma((2, chips)),
            dma((2, chips)),
            dma((group,)),
            dma((group,)),
        ],
        compiler_params=pltpu.CompilerParams(
            collective_id=0, has_side_effects=True, vmem_limit_bytes=32 * 1024 * 1024
        ),
        cost_estimate=pl.CostEstimate(
            flops=2 * features * width * rows, bytes_accessed=2 * features * width, transcendentals=0
        ),
        name="power_backward",
    )(queries, keys, values, out_grad, prefix_states)


def solution(mesh):
    return jax.shard_map(
        body,
        mesh=mesh,
        in_specs=(
            P("query", "context", None),
            P("context", None),
            P("context", None),
            P("query", "context", None),
            P("context", None, None),
        ),
        out_specs=(
            P("query", "context", None),
            P("context", "query", None),
            P("context", "query", None),
        ),
        check_vma=False,
    )
```

```python
import functools

import jax
import jax.numpy as jnp
import numpy as np
from jax import lax
from jax.experimental import pallas as pl
from jax.experimental.pallas import tpu as pltpu
from jax.sharding import PartitionSpec as P

MESH = pl.DeviceIdType.MESH
NT = (((1,), (1,)), ((), ()))
NN = (((1,), (0,)), ((), ()))


def dot(a, b, dims):
    return lax.dot_general(a, b, dims, preferred_element_type=jnp.float32)


def chunk_count(features, most=4):
    for count in range(most, 0, -1):
        if features % (16 * count) == 0:
            return count
    return 1


def kernel(
    q_ref, k_ref, v_ref, g_ref, p_ref, dq_ref, dk_ref, dv_ref,
    kk, vv, qb, gb, pb, fb, xt, red, acc, sb, rb,
    local_sem, p_sem, kv_send, kv_recv, z_send, z_recv, x_send, x_recv,
):
    heads = lax.axis_size("query")
    chips = lax.axis_size("context") // 2
    group = 2 * heads
    h = lax.axis_index("query")
    place = lax.axis_index("context")
    z, core = place // 2, place % 2
    me = core * heads + h
    rows, width = q_ref.shape[1], q_ref.shape[2]
    features = p_ref.shape[1]
    scale = 1.0 / (width * rows)
    share = rows // heads
    chunks = chunk_count(features)
    chunk = features // chunks

    loads = [
        pltpu.make_async_copy(q_ref.at[0], qb.at[0], local_sem.at[0]),
        pltpu.make_async_copy(g_ref.at[0], gb.at[0], local_sem.at[1]),
        pltpu.make_async_copy(k_ref, kk.at[core], local_sem.at[2]),
        pltpu.make_async_copy(v_ref, vv.at[core], local_sem.at[3]),
    ]
    for load in loads:
        load.start()
    for n in range(chunks):
        part = pl.ds(n * chunk, chunk)
        pltpu.make_async_copy(p_ref.at[0, part], pb.at[part], p_sem.at[n]).start()

    barrier = pltpu.get_barrier_semaphore()

    def peer(offset):
        other = lax.rem(me + offset, group)
        return {"query": other % heads, "context": 2 * z + other // heads}

    for offset in range(1, group):
        pl.semaphore_signal(barrier, inc=1, device_id=peer(offset), device_id_type=MESH)
    for step in range(1, chips):
        @pl.when(z + step < chips)
        def _():
            pl.semaphore_signal(
                barrier, inc=1, device_id={"context": place + 2 * step}, device_id_type=MESH
            )
    pl.semaphore_wait(barrier, group - 1 + z)

    def down(step):
        return [
            pltpu.make_async_remote_copy(
                src_ref=src.at[0],
                dst_ref=dst.at[step],
                send_sem=z_send.at[which, step],
                recv_sem=z_recv.at[which, step],
                device_id={"context": place - 2 * step},
                device_id_type=MESH,
            )
            for which, (src, dst) in enumerate(((q_ref, qb), (g_ref, gb)))
        ]

    for step in range(chips - 1, 0, -1):
        @pl.when(z >= step)
        def _():
            for copy in down(step):
                copy.start()

    kv = [
        pltpu.make_async_remote_copy(
            src_ref=src,
            dst_ref=dst.at[core],
            send_sem=kv_send.at[which],
            recv_sem=kv_recv.at[which],
            device_id={"context": place + 1 - 2 * core},
            device_id_type=MESH,
        )
        for which, (src, dst) in enumerate(((k_ref, kk), (v_ref, vv)))
    ]
    for copy in kv:
        copy.start()
    for load in loads:
        load.wait()

    q_own, g_own = qb[0], gb[0]
    xt[...] = q_own.astype(jnp.float32).T
    spot = lax.broadcasted_iota(jnp.int32, (8, rows), 0)

    def expand(n, carry):
        part = pl.ds(pl.multiple_of(n * chunk, chunk), chunk)
        pltpu.make_async_copy(p_ref.at[0, part], pb.at[part], p_sem.at[n]).wait()
        fb[part, :] = dot(pb[part, :], g_own, NT)
        return carry

    lax.fori_loop(0, chunks, expand, 0)
    total = jnp.zeros((width, rows), jnp.float32)
    cross = []
    for tile in range(width // 8):
        length = width - 8 * tile

        def one(r, total, tile=tile, length=length):
            i = 8 * tile + r
            begin = i * width - (i * (i - 1)) // 2 - r
            feat = fb[pl.ds(begin, length), :]
            weight = jnp.where(spot < r, 0.0, jnp.where(spot == r, np.float32(np.sqrt(0.5)), 1.0))
            head = feat[:8] * weight
            feat = jnp.concatenate([head, feat[8:]], axis=0) if length > 8 else head
            row = xt[pl.ds(i, 1), :]
            x_tile = xt[8 * tile:, :]
            red[i] = jnp.sum((feat * x_tile).reshape(length // 8, 8, rows), axis=0)
            return total + feat * row

        total = lax.fori_loop(0, 8, one, total)
        cross.append(total[:8])
        total = total[8:]
    cross_t = jnp.concatenate(cross, axis=0) + jnp.sum(red[...], axis=1)
    cross_q = (scale * np.sqrt(2.0)) * cross_t.T

    for copy in kv:
        copy.wait()
    keys = kk[...].reshape(2 * rows, width)
    vals = vv[...].reshape(2 * rows, width)

    def weights(q, g):
        score = dot(keys, q, NT)
        return scale * score * score, (2.0 * scale) * score * dot(vals, g, NT)

    attn, slope = weights(q_own, g_own)
    key_at = lax.broadcasted_iota(jnp.int32, (2 * rows, rows), 0)
    query_at = lax.broadcasted_iota(jnp.int32, (2 * rows, rows), 1) + core * rows
    causal = key_at <= query_at
    attn = jnp.where(causal, attn, 0.0).astype(jnp.bfloat16)
    slope = jnp.where(causal, slope, 0.0).astype(jnp.bfloat16)
    acc[:, :width] = dot(slope, q_own, NN)
    acc[:, width:] = dot(attn, g_own, NN)
    own_score = dot(q_own, kk[core], NT)
    own_slope = (2.0 * scale) * own_score * dot(g_own, vv[core], NT)
    own_causal = lax.broadcasted_iota(jnp.int32, (rows, rows), 1) <= lax.broadcasted_iota(
        jnp.int32, (rows, rows), 0
    )
    own_slope = jnp.where(own_causal, own_slope, 0.0).astype(jnp.bfloat16)
    dq_ref[0] = (dot(own_slope, kk[core], NN) + cross_q).astype(dq_ref.dtype)

    for step in range(1, chips):
        @pl.when(z + step < chips)
        def _():
            for copy in down(step):
                copy.wait_recv()
            q, g = qb[step], gb[step]
            attn, slope = weights(q, g)
            acc[:, :width] += dot(slope.astype(jnp.bfloat16), q, NN)
            acc[:, width:] += dot(attn.astype(jnp.bfloat16), g, NN)

    sb[...] = acc[...].astype(jnp.bfloat16).reshape(group, share, 2 * width)
    swaps = []
    for offset in range(1, group):
        other = lax.rem(me + offset, group)
        copy = pltpu.make_async_remote_copy(
            src_ref=sb.at[other],
            dst_ref=rb.at[offset],
            send_sem=x_send.at[offset],
            recv_sem=x_recv.at[offset],
            device_id=peer(offset),
            device_id_type=MESH,
        )
        copy.start()
        swaps.append(copy)
    mine = acc[pl.ds(pl.multiple_of(me * share, share), share), :]
    for offset, copy in enumerate(swaps, 1):
        copy.wait_recv()
        mine = mine + rb[offset].astype(jnp.float32)
    dk_ref[0] = mine[:, :width].astype(dk_ref.dtype)
    dv_ref[0] = mine[:, width:].astype(dv_ref.dtype)

    for copy in swaps:
        copy.wait_send()
    for step in range(1, chips):
        @pl.when(z >= step)
        def _():
            for copy in down(step):
                copy.wait_send()


def body(queries, keys, values, out_grad, prefix_states):
    heads = lax.axis_size("query")
    chips = lax.axis_size("context") // 2
    group = 2 * heads
    rows, width = keys.shape
    features = prefix_states.shape[1]
    share = rows // heads
    chunks = chunk_count(features)
    half = jax.ShapeDtypeStruct((1, share, width), jnp.bfloat16)
    dma = pltpu.SemaphoreType.DMA
    return pl.pallas_call(
        kernel,
        out_shape=(jax.ShapeDtypeStruct(queries.shape, jnp.bfloat16), half, half),
        in_specs=[pl.BlockSpec(memory_space=pl.ANY)] * 5,
        out_specs=[pl.BlockSpec(memory_space=pltpu.VMEM)] * 3,
        scratch_shapes=[
            pltpu.VMEM((2, rows, width), jnp.bfloat16),
            pltpu.VMEM((2, rows, width), jnp.bfloat16),
            pltpu.VMEM((chips, rows, width), jnp.bfloat16),
            pltpu.VMEM((chips, rows, width), jnp.bfloat16),
            pltpu.VMEM((features, width), jnp.bfloat16),
            pltpu.VMEM((features, rows), jnp.float32),
            pltpu.VMEM((width, rows), jnp.float32),
            pltpu.VMEM((width, 8, rows), jnp.float32),
            pltpu.VMEM((2 * rows, 2 * width), jnp.float32),
            pltpu.VMEM((group, share, 2 * width), jnp.bfloat16),
            pltpu.VMEM((group, share, 2 * width), jnp.bfloat16),
            dma((4,)),
            dma((chunks,)),
            dma((2,)),
            dma((2,)),
            dma((2, chips)),
            dma((2, chips)),
            dma((group,)),
            dma((group,)),
        ],
        compiler_params=pltpu.CompilerParams(
            collective_id=0, has_side_effects=True, vmem_limit_bytes=63 * 1024 * 1024
        ),
        cost_estimate=pl.CostEstimate(
            flops=2 * features * width * rows, bytes_accessed=2 * features * width, transcendentals=0
        ),
        name="power_backward",
    )(queries, keys, values, out_grad, prefix_states)


def solution(mesh):
    return jax.shard_map(
        body,
        mesh=mesh,
        in_specs=(
            P("query", "context", None),
            P("context", None),
            P("context", None),
            P("query", "context", None),
            P("context", None, None),
        ),
        out_specs=(
            P("query", "context", None),
            P("context", "query", None),
            P("context", "query", None),
        ),
        check_vma=False,
    )
```

```python
import functools

import jax
import jax.numpy as jnp
import numpy as np
from jax import lax
from jax.experimental import pallas as pl
from jax.experimental.pallas import tpu as pltpu
from jax.sharding import PartitionSpec as P

MESH = pl.DeviceIdType.MESH
NT = (((1,), (1,)), ((), ()))
NN = (((1,), (0,)), ((), ()))


def dot(a, b, dims):
    return lax.dot_general(a, b, dims, preferred_element_type=jnp.float32)


def chunk_count(features, most=4):
    for count in range(most, 0, -1):
        if features % (16 * count) == 0:
            return count
    return 1


def block_batch(chips, most=4):
    return max(size for size in range(1, most + 1) if chips % size == 0)


def place(dq_in, dkv_in, dq_out, dk_out, dv_out, sems):
    copies = [
        pltpu.make_async_copy(src, dst, sems.at[n])
        for n, (src, dst) in enumerate(
            ((dq_in, dq_out), (dkv_in.at[0], dk_out.at[0]), (dkv_in.at[1], dv_out.at[0]))
        )
    ]
    for copy in copies:
        copy.start()
    for copy in copies:
        copy.wait()


def kernel(
    q_ref, k_ref, v_ref, g_ref, p_ref, dq_ref, dkv_ref,
    dqb, dkvb, kk, vv, qb, gb, pb, fb, xt, red, acc, sb, rb,
    out_sem, local_sem, p_sem, kv_send, kv_recv, z_send, z_recv, x_send, x_recv,
):
    heads = lax.axis_size("query")
    chips = lax.axis_size("context") // 2
    group = 2 * heads
    h = lax.axis_index("query")
    spot_at = lax.axis_index("context")
    z, core = spot_at // 2, spot_at % 2
    me = core * heads + h
    rows, width = q_ref.shape[1], q_ref.shape[2]
    features = p_ref.shape[1]
    scale = 1.0 / (width * rows)
    share = rows // heads
    chunks = chunk_count(features)
    chunk = features // chunks

    loads = [
        pltpu.make_async_copy(q_ref.at[0], qb.at[0], local_sem.at[0]),
        pltpu.make_async_copy(g_ref.at[0], gb.at[0], local_sem.at[1]),
        pltpu.make_async_copy(k_ref, kk.at[core], local_sem.at[2]),
        pltpu.make_async_copy(v_ref, vv.at[core], local_sem.at[3]),
    ]
    for load in loads:
        load.start()
    for n in range(chunks):
        part = pl.ds(n * chunk, chunk)
        pltpu.make_async_copy(p_ref.at[0, part], pb.at[part], p_sem.at[n]).start()

    barrier = pltpu.get_barrier_semaphore()

    def peer(offset):
        other = lax.rem(me + offset, group)
        return {"query": other % heads, "context": 2 * z + other // heads}

    for offset in range(1, group):
        pl.semaphore_signal(barrier, inc=1, device_id=peer(offset), device_id_type=MESH)
    for step in range(1, chips):
        @pl.when(z + step < chips)
        def _():
            pl.semaphore_signal(
                barrier, inc=1, device_id={"context": spot_at + 2 * step}, device_id_type=MESH
            )
    pl.semaphore_wait(barrier, group - 1 + z)

    def down(step):
        return [
            pltpu.make_async_remote_copy(
                src_ref=src.at[0],
                dst_ref=dst.at[step],
                send_sem=z_send.at[which, step],
                recv_sem=z_recv.at[which, step],
                device_id={"context": spot_at - 2 * step},
                device_id_type=MESH,
            )
            for which, (src, dst) in enumerate(((q_ref, qb), (g_ref, gb)))
        ]

    for step in range(chips - 1, 0, -1):
        @pl.when(z >= step)
        def _():
            for copy in down(step):
                copy.start()

    kv = [
        pltpu.make_async_remote_copy(
            src_ref=src,
            dst_ref=dst.at[core],
            send_sem=kv_send.at[which],
            recv_sem=kv_recv.at[which],
            device_id={"context": spot_at + 1 - 2 * core},
            device_id_type=MESH,
        )
        for which, (src, dst) in enumerate(((k_ref, kk), (v_ref, vv)))
    ]
    for copy in kv:
        copy.start()
    for step in range(1, chips):
        @pl.when(z + step >= chips)
        def _():
            qb[step] = jnp.zeros((rows, width), jnp.bfloat16)
            gb[step] = jnp.zeros((rows, width), jnp.bfloat16)
    for load in loads:
        load.wait()

    q_own, g_own = qb[0], gb[0]
    xt[...] = q_own.astype(jnp.float32).T
    spot = lax.broadcasted_iota(jnp.int32, (8, rows), 0)

    def expand(n, carry):
        part = pl.ds(pl.multiple_of(n * chunk, chunk), chunk)
        pltpu.make_async_copy(p_ref.at[0, part], pb.at[part], p_sem.at[n]).wait()
        fb[part, :] = dot(pb[part, :], g_own, NT)
        return carry

    lax.fori_loop(0, chunks, expand, 0)
    total = jnp.zeros((width, rows), jnp.float32)
    cross = []
    for tile in range(width // 8):
        length = width - 8 * tile

        def one(r, total, tile=tile, length=length):
            i = 8 * tile + r
            begin = i * width - (i * (i - 1)) // 2 - r
            feat = fb[pl.ds(begin, length), :]
            weight = jnp.where(spot < r, 0.0, jnp.where(spot == r, np.float32(np.sqrt(0.5)), 1.0))
            head = feat[:8] * weight
            feat = jnp.concatenate([head, feat[8:]], axis=0) if length > 8 else head
            row = xt[pl.ds(i, 1), :]
            x_tile = xt[8 * tile:, :]
            red[i] = jnp.sum((feat * x_tile).reshape(length // 8, 8, rows), axis=0)
            return total + feat * row

        total = lax.fori_loop(0, 8, one, total, unroll=2)
        cross.append(total[:8])
        total = total[8:]
    cross_t = jnp.concatenate(cross, axis=0) + jnp.sum(red[...], axis=1)
    cross_q = (scale * np.sqrt(2.0)) * cross_t.T

    for copy in kv:
        copy.wait()
    keys = kk[...].reshape(2 * rows, width)
    vals = vv[...].reshape(2 * rows, width)

    def weights(q, g):
        score = dot(keys, q, NT)
        return scale * score * score, (2.0 * scale) * score * dot(vals, g, NT)

    own_score = dot(q_own, kk[core], NT)
    own_slope = (2.0 * scale) * own_score * dot(g_own, vv[core], NT)
    own_causal = lax.broadcasted_iota(jnp.int32, (rows, rows), 1) <= lax.broadcasted_iota(
        jnp.int32, (rows, rows), 0
    )
    own_slope = jnp.where(own_causal, own_slope, 0.0).astype(jnp.bfloat16)
    dqb[0] = (dot(own_slope, kk[core], NN) + cross_q).astype(dqb.dtype)
    dq_out = pltpu.make_async_copy(dqb, dq_ref, out_sem.at[0])
    dq_out.start()

    batch = block_batch(chips)
    key_at = lax.broadcasted_iota(jnp.int32, (2 * rows, batch * rows), 0)
    query_at = lax.broadcasted_iota(jnp.int32, (2 * rows, batch * rows), 1)
    causal = key_at <= jnp.where(query_at < rows, query_at + core * rows, 2 * rows)

    def arrive(step):
        @pl.when(z + step < chips)
        def _():
            for copy in down(step):
                copy.wait_recv()

    def key_terms(first, masked):
        part = pl.ds(first, batch)
        q = qb[part].reshape(batch * rows, width)
        g = gb[part].reshape(batch * rows, width)
        attn, slope = weights(q, g)
        if masked:
            attn, slope = jnp.where(causal, attn, 0.0), jnp.where(causal, slope, 0.0)
        return dot(slope.astype(jnp.bfloat16), q, NN), dot(attn.astype(jnp.bfloat16), g, NN)

    for step in range(1, batch):
        arrive(step)
    acc[:, :width], acc[:, width:] = key_terms(0, True)

    def more(n, carry):
        for step in range(batch):
            arrive(n * batch + step)
        to_keys, to_values = key_terms(n * batch, False)
        acc[:, :width] += to_keys
        acc[:, width:] += to_values
        return carry

    if chips > batch:
        lax.fori_loop(1, chips // batch, more, 0)

    sb[...] = acc[...].astype(jnp.bfloat16).reshape(group, share, 2 * width)
    swaps = []
    for offset in range(1, group):
        other = lax.rem(me + offset, group)
        copy = pltpu.make_async_remote_copy(
            src_ref=sb.at[other],
            dst_ref=rb.at[offset],
            send_sem=x_send.at[offset],
            recv_sem=x_recv.at[offset],
            device_id=peer(offset),
            device_id_type=MESH,
        )
        copy.start()
        swaps.append(copy)
    mine = acc[pl.ds(pl.multiple_of(me * share, share), share), :]
    for offset, copy in enumerate(swaps, 1):
        copy.wait_recv()
        mine = mine + rb[offset].astype(jnp.float32)
    dkvb[0] = mine[:, :width].astype(dkvb.dtype)
    dkvb[1] = mine[:, width:].astype(dkvb.dtype)
    dkv_out = pltpu.make_async_copy(dkvb, dkv_ref, out_sem.at[1])
    dkv_out.start()

    for copy in swaps:
        copy.wait_send()
    for step in range(1, chips):
        @pl.when(z >= step)
        def _():
            for copy in down(step):
                copy.wait_send()
    dq_out.wait()
    dkv_out.wait()


def body(queries, keys, values, out_grad, prefix_states):
    heads = lax.axis_size("query")
    chips = lax.axis_size("context") // 2
    group = 2 * heads
    rows, width = keys.shape
    features = prefix_states.shape[1]
    share = rows // heads
    chunks = chunk_count(features)
    whole = jax.ShapeDtypeStruct(queries.shape, jnp.bfloat16)
    half = jax.ShapeDtypeStruct((1, share, width), jnp.bfloat16)
    dma = pltpu.SemaphoreType.DMA
    grad_q, grad_kv = pl.pallas_call(
        kernel,
        out_shape=(whole, jax.ShapeDtypeStruct((2, share, width), jnp.bfloat16)),
        in_specs=[pl.BlockSpec(memory_space=pl.ANY)] * 5,
        out_specs=[pl.BlockSpec(memory_space=pl.ANY)] * 2,
        scratch_shapes=[
            pltpu.VMEM(queries.shape, jnp.bfloat16),
            pltpu.VMEM((2, share, width), jnp.bfloat16),
            pltpu.VMEM((2, rows, width), jnp.bfloat16),
            pltpu.VMEM((2, rows, width), jnp.bfloat16),
            pltpu.VMEM((chips, rows, width), jnp.bfloat16),
            pltpu.VMEM((chips, rows, width), jnp.bfloat16),
            pltpu.VMEM((features, width), jnp.bfloat16),
            pltpu.VMEM((features, rows), jnp.float32),
            pltpu.VMEM((width, rows), jnp.float32),
            pltpu.VMEM((width, 8, rows), jnp.float32),
            pltpu.VMEM((2 * rows, 2 * width), jnp.float32),
            pltpu.VMEM((group, share, 2 * width), jnp.bfloat16),
            pltpu.VMEM((group, share, 2 * width), jnp.bfloat16),
            dma((2,)),
            dma((4,)),
            dma((chunks,)),
            dma((2,)),
            dma((2,)),
            dma((2, chips)),
            dma((2, chips)),
            dma((group,)),
            dma((group,)),
        ],
        compiler_params=pltpu.CompilerParams(
            collective_id=0, has_side_effects=True, vmem_limit_bytes=63 * 1024 * 1024
        ),
        cost_estimate=pl.CostEstimate(
            flops=2 * features * width * rows, bytes_accessed=2 * features * width, transcendentals=0
        ),
        name="power_backward",
    )(queries, keys, values, out_grad, prefix_states)
    return pl.pallas_call(
        place,
        out_shape=(whole, half, half),
        in_specs=[pl.BlockSpec(memory_space=pl.ANY)] * 2,
        out_specs=[pl.BlockSpec(memory_space=pl.ANY)] * 3,
        scratch_shapes=[dma((3,))],
        compiler_params=pltpu.CompilerParams(vmem_limit_bytes=63 * 1024 * 1024),
        name="place_results",
    )(grad_q, grad_kv)


def solution(mesh):
    return jax.shard_map(
        body,
        mesh=mesh,
        in_specs=(
            P("query", "context", None),
            P("context", None),
            P("context", None),
            P("query", "context", None),
            P("context", None, None),
        ),
        out_specs=(
            P("query", "context", None),
            P("context", "query", None),
            P("context", "query", None),
        ),
        check_vma=False,
    )
```

```python
import functools

import jax
import jax.numpy as jnp
import numpy as np
from jax import lax
from jax.experimental import pallas as pl
from jax.experimental.pallas import tpu as pltpu
from jax.sharding import PartitionSpec as P

MESH = pl.DeviceIdType.MESH
NT = (((1,), (1,)), ((), ()))
NN = (((1,), (0,)), ((), ()))


def dot(a, b, dims):
    return lax.dot_general(a, b, dims, preferred_element_type=jnp.float32)


def chunk_count(features, most=4):
    for count in range(most, 0, -1):
        if features % (16 * count) == 0:
            return count
    return 1


def block_batch(chips, most=4):
    return max(size for size in range(1, most + 1) if chips % size == 0)


def place(dq_in, dkv_in, dq_out, dk_out, dv_out, dq, dkv, sems):
    fetch = [
        pltpu.make_async_copy(dkv_in, dkv, sems.at[0]),
        pltpu.make_async_copy(dq_in, dq, sems.at[1]),
    ]
    put = [
        pltpu.make_async_copy(dkv.at[0], dk_out.at[0], sems.at[2]),
        pltpu.make_async_copy(dkv.at[1], dv_out.at[0], sems.at[3]),
        pltpu.make_async_copy(dq, dq_out, sems.at[4]),
    ]
    for copy in fetch:
        copy.start()
    fetch[0].wait()
    put[0].start()
    put[1].start()
    fetch[1].wait()
    put[2].start()
    for copy in put:
        copy.wait()


def kernel(
    q_ref, k_ref, v_ref, g_ref, p_ref, dq_ref, dkv_ref,
    dqb, dkvb, kk, vv, qb, gb, pb, fb, xt, red, acc, sb, rb,
    out_sem, local_sem, p_sem, kv_send, kv_recv, z_send, z_recv, x_send, x_recv,
):
    heads = lax.axis_size("query")
    chips = lax.axis_size("context") // 2
    group = 2 * heads
    h = lax.axis_index("query")
    spot_at = lax.axis_index("context")
    z, core = spot_at // 2, spot_at % 2
    me = core * heads + h
    rows, width = q_ref.shape[1], q_ref.shape[2]
    features = p_ref.shape[1]
    scale = 1.0 / (width * rows)
    share = rows // heads
    chunks = chunk_count(features)
    chunk = features // chunks

    loads = [
        pltpu.make_async_copy(q_ref.at[0], qb.at[0], local_sem.at[0]),
        pltpu.make_async_copy(g_ref.at[0], gb.at[0], local_sem.at[1]),
        pltpu.make_async_copy(k_ref, kk.at[core], local_sem.at[2]),
        pltpu.make_async_copy(v_ref, vv.at[core], local_sem.at[3]),
    ]
    for load in loads:
        load.start()
    for n in range(chunks):
        part = pl.ds(n * chunk, chunk)
        pltpu.make_async_copy(p_ref.at[0, part], pb.at[part], p_sem.at[n]).start()

    barrier = pltpu.get_barrier_semaphore()

    def peer(offset):
        other = lax.rem(me + offset, group)
        return {"query": other % heads, "context": 2 * z + other // heads}

    for offset in range(1, group):
        pl.semaphore_signal(barrier, inc=1, device_id=peer(offset), device_id_type=MESH)

    @pl.when(z + 1 < chips)
    def _():
        pl.semaphore_signal(barrier, inc=1, device_id={"context": spot_at + 2}, device_id_type=MESH)

    pl.semaphore_wait(barrier, group - 1 + jnp.minimum(z, 1))

    def hop(slot, which):
        source, slots = ((q_ref, qb), (g_ref, gb))[which]
        own = isinstance(slot, int) and slot == 0
        return pltpu.make_async_remote_copy(
            src_ref=source.at[0] if own else slots.at[slot],
            dst_ref=slots.at[slot + 1],
            send_sem=z_send.at[which, slot],
            recv_sem=z_recv.at[which, slot],
            device_id={"context": spot_at - 2},
            device_id_type=MESH,
        )

    def start_own(which):
        @pl.when(z > 0)
        def _():
            hop(0, which).start()

    def forward(slot, which):
        @pl.when((z > 0) & (z + slot < chips))
        def _():
            hop(slot - 1, which).wait_recv()
            hop(slot, which).start()

    start_own(0)
    kv = [
        pltpu.make_async_remote_copy(
            src_ref=src,
            dst_ref=dst.at[core],
            send_sem=kv_send.at[which],
            recv_sem=kv_recv.at[which],
            device_id={"context": spot_at + 1 - 2 * core},
            device_id_type=MESH,
        )
        for which, (src, dst) in enumerate(((k_ref, kk), (v_ref, vv)))
    ]
    for copy in kv:
        copy.start()
    for step in range(1, chips):
        @pl.when(z + step >= chips)
        def _():
            qb[step] = jnp.zeros((rows, width), jnp.bfloat16)
            gb[step] = jnp.zeros((rows, width), jnp.bfloat16)
    for load in loads:
        load.wait()

    q_own, g_own = qb[0], gb[0]
    xt[...] = q_own.astype(jnp.float32).T
    spot = lax.broadcasted_iota(jnp.int32, (8, rows), 0)

    def expand(n, carry):
        part = pl.ds(pl.multiple_of(n * chunk, chunk), chunk)
        pltpu.make_async_copy(p_ref.at[0, part], pb.at[part], p_sem.at[n]).wait()
        fb[part, :] = dot(pb[part, :], g_own, NT)
        return carry

    lax.fori_loop(0, chunks // 2, expand, 0)
    start_own(1)
    lax.fori_loop(chunks // 2, chunks, expand, 0)
    between = {0: (1, 0), 3: (1, 1), 7: (2, 0), width // 8 - 1: (2, 1)}
    total = jnp.zeros((width, rows), jnp.float32)
    cross = []
    for tile in range(width // 8):
        length = width - 8 * tile
        if tile in between and between[tile][0] < chips - 1:
            forward(*between[tile])

        def one(r, total, tile=tile, length=length):
            i = 8 * tile + r
            begin = i * width - (i * (i - 1)) // 2 - r
            feat = fb[pl.ds(begin, length), :]
            weight = jnp.where(spot < r, 0.0, jnp.where(spot == r, np.float32(np.sqrt(0.5)), 1.0))
            head = feat[:8] * weight
            feat = jnp.concatenate([head, feat[8:]], axis=0) if length > 8 else head
            row = xt[pl.ds(i, 1), :]
            x_tile = xt[8 * tile:, :]
            red[i] = jnp.sum((feat * x_tile).reshape(length // 8, 8, rows), axis=0)
            return total + feat * row

        total = lax.fori_loop(0, 8, one, total, unroll=2)
        cross.append(total[:8])
        total = total[8:]
    cross_t = jnp.concatenate(cross, axis=0) + jnp.sum(red[...], axis=1)
    cross_q = (scale * np.sqrt(2.0)) * cross_t.T

    for copy in kv:
        copy.wait()
    keys = kk[...].reshape(2 * rows, width)
    vals = vv[...].reshape(2 * rows, width)

    def weights(q, g):
        score = dot(keys, q, NT)
        return scale * score * score, (2.0 * scale) * score * dot(vals, g, NT)

    own_score = dot(q_own, kk[core], NT)
    own_slope = (2.0 * scale) * own_score * dot(g_own, vv[core], NT)
    own_causal = lax.broadcasted_iota(jnp.int32, (rows, rows), 1) <= lax.broadcasted_iota(
        jnp.int32, (rows, rows), 0
    )
    own_slope = jnp.where(own_causal, own_slope, 0.0).astype(jnp.bfloat16)
    dqb[0] = (dot(own_slope, kk[core], NN) + cross_q).astype(dqb.dtype)
    dq_out = pltpu.make_async_copy(dqb, dq_ref, out_sem.at[0])
    dq_out.start()

    batch = block_batch(chips)
    key_at = lax.broadcasted_iota(jnp.int32, (2 * rows, batch * rows), 0)
    query_at = lax.broadcasted_iota(jnp.int32, (2 * rows, batch * rows), 1)
    causal = key_at <= jnp.where(query_at < rows, query_at + core * rows, 2 * rows)

    def arrive(step):
        @pl.when(z == 0)
        def _():
            for which in range(2):
                hop(step - 1, which).wait_recv()

    def key_terms(first, masked):
        part = pl.ds(first, batch)
        q = qb[part].reshape(batch * rows, width)
        g = gb[part].reshape(batch * rows, width)
        attn, slope = weights(q, g)
        if masked:
            attn, slope = jnp.where(causal, attn, 0.0), jnp.where(causal, slope, 0.0)
        return dot(slope.astype(jnp.bfloat16), q, NN), dot(attn.astype(jnp.bfloat16), g, NN)

    def rest(slot, carry):
        forward(slot, 0)
        forward(slot, 1)
        return carry

    if chips > 4:
        lax.fori_loop(3, chips - 1, rest, 0)
    for step in range(1, batch):
        arrive(step)
    acc[:, :width], acc[:, width:] = key_terms(0, True)

    def more(n, carry):
        for step in range(batch):
            arrive(n * batch + step)
        to_keys, to_values = key_terms(n * batch, False)
        acc[:, :width] += to_keys
        acc[:, width:] += to_values
        return carry

    if chips > batch:
        lax.fori_loop(1, chips // batch, more, 0)

    sb[...] = acc[...].astype(jnp.bfloat16).reshape(group, share, 2 * width)
    swaps = []
    for offset in range(1, group):
        other = lax.rem(me + offset, group)
        copy = pltpu.make_async_remote_copy(
            src_ref=sb.at[other],
            dst_ref=rb.at[offset],
            send_sem=x_send.at[offset],
            recv_sem=x_recv.at[offset],
            device_id=peer(offset),
            device_id_type=MESH,
        )
        copy.start()
        swaps.append(copy)
    mine = acc[pl.ds(pl.multiple_of(me * share, share), share), :]
    for offset, copy in enumerate(swaps, 1):
        copy.wait_recv()
        mine = mine + rb[offset].astype(jnp.float32)
    dkvb[0] = mine[:, :width].astype(dkvb.dtype)
    dkvb[1] = mine[:, width:].astype(dkvb.dtype)
    dkv_out = pltpu.make_async_copy(dkvb, dkv_ref, out_sem.at[1])
    dkv_out.start()

    for copy in swaps:
        copy.wait_send()
    for slot in range(chips - 1):
        @pl.when((z > 0) & (z + slot < chips))
        def _():
            for which in range(2):
                hop(slot, which).wait_send()
    dq_out.wait()
    dkv_out.wait()


def body(queries, keys, values, out_grad, prefix_states):
    heads = lax.axis_size("query")
    chips = lax.axis_size("context") // 2
    group = 2 * heads
    rows, width = keys.shape
    features = prefix_states.shape[1]
    share = rows // heads
    chunks = chunk_count(features)
    whole = jax.ShapeDtypeStruct(queries.shape, jnp.bfloat16)
    half = jax.ShapeDtypeStruct((1, share, width), jnp.bfloat16)
    dma = pltpu.SemaphoreType.DMA
    grad_q, grad_kv = pl.pallas_call(
        kernel,
        out_shape=(whole, jax.ShapeDtypeStruct((2, share, width), jnp.bfloat16)),
        in_specs=[pl.BlockSpec(memory_space=pl.ANY)] * 5,
        out_specs=[pl.BlockSpec(memory_space=pl.ANY)] * 2,
        scratch_shapes=[
            pltpu.VMEM(queries.shape, jnp.bfloat16),
            pltpu.VMEM((2, share, width), jnp.bfloat16),
            pltpu.VMEM((2, rows, width), jnp.bfloat16),
            pltpu.VMEM((2, rows, width), jnp.bfloat16),
            pltpu.VMEM((chips, rows, width), jnp.bfloat16),
            pltpu.VMEM((chips, rows, width), jnp.bfloat16),
            pltpu.VMEM((features, width), jnp.bfloat16),
            pltpu.VMEM((features, rows), jnp.float32),
            pltpu.VMEM((width, rows), jnp.float32),
            pltpu.VMEM((width, 8, rows), jnp.float32),
            pltpu.VMEM((2 * rows, 2 * width), jnp.float32),
            pltpu.VMEM((group, share, 2 * width), jnp.bfloat16),
            pltpu.VMEM((group, share, 2 * width), jnp.bfloat16),
            dma((2,)),
            dma((4,)),
            dma((chunks,)),
            dma((2,)),
            dma((2,)),
            dma((2, chips)),
            dma((2, chips)),
            dma((group,)),
            dma((group,)),
        ],
        compiler_params=pltpu.CompilerParams(
            collective_id=0, has_side_effects=True, vmem_limit_bytes=63 * 1024 * 1024
        ),
        cost_estimate=pl.CostEstimate(
            flops=2 * features * width * rows, bytes_accessed=2 * features * width, transcendentals=0
        ),
        name="power_backward",
    )(queries, keys, values, out_grad, prefix_states)
    return pl.pallas_call(
        place,
        out_shape=(whole, half, half),
        in_specs=[pl.BlockSpec(memory_space=pl.ANY)] * 2,
        out_specs=[pl.BlockSpec(memory_space=pl.ANY)] * 3,
        scratch_shapes=[
            pltpu.VMEM(queries.shape, jnp.bfloat16),
            pltpu.VMEM((2, share, width), jnp.bfloat16),
            dma((5,)),
        ],
        compiler_params=pltpu.CompilerParams(vmem_limit_bytes=63 * 1024 * 1024),
        name="place_results",
    )(grad_q, grad_kv)


def solution(mesh):
    return jax.shard_map(
        body,
        mesh=mesh,
        in_specs=(
            P("query", "context", None),
            P("context", None),
            P("context", None),
            P("query", "context", None),
            P("context", None, None),
        ),
        out_specs=(
            P("query", "context", None),
            P("context", "query", None),
            P("context", "query", None),
        ),
        check_vma=False,
    )
```

```python
import functools

import jax
import jax.numpy as jnp
import numpy as np
from jax import lax
from jax.experimental import pallas as pl
from jax.experimental.pallas import tpu as pltpu
from jax.sharding import PartitionSpec as P

MESH = pl.DeviceIdType.MESH
NT = (((1,), (1,)), ((), ()))
NN = (((1,), (0,)), ((), ()))


def dot(a, b, dims):
    return lax.dot_general(a, b, dims, preferred_element_type=jnp.float32)


def chunk_count(features, most=4):
    for count in range(most, 0, -1):
        if features % (16 * count) == 0:
            return count
    return 1


def block_batch(chips, most=4):
    return max(size for size in range(1, most + 1) if chips % size == 0)


def place(dq_in, dkv_in, dq_out, dk_out, dv_out, sems):
    copies = [
        pltpu.make_async_copy(src, dst, sems.at[n])
        for n, (src, dst) in enumerate(
            ((dq_in, dq_out), (dkv_in.at[0], dk_out.at[0]), (dkv_in.at[1], dv_out.at[0]))
        )
    ]
    for copy in copies:
        copy.start()
    for copy in copies:
        copy.wait()


def kernel(
    q_ref, k_ref, v_ref, g_ref, p_ref, dq_ref, dkv_ref,
    dqb, dkvb, kk, vv, qb, gb, pb, fb, xt, red, acc, sb, rb,
    out_sem, local_sem, p_sem, kv_send, kv_recv, z_send, z_recv, x_send, x_recv,
):
    heads = lax.axis_size("query")
    chips = lax.axis_size("context") // 2
    group = 2 * heads
    h = lax.axis_index("query")
    spot_at = lax.axis_index("context")
    z, core = spot_at // 2, spot_at % 2
    me = core * heads + h
    rows, width = q_ref.shape[1], q_ref.shape[2]
    features = p_ref.shape[1]
    scale = 1.0 / (width * rows)
    share = rows // heads
    chunks = chunk_count(features)
    chunk = features // chunks

    loads = [
        pltpu.make_async_copy(q_ref.at[0], qb.at[0], local_sem.at[0]),
        pltpu.make_async_copy(g_ref.at[0], gb.at[0], local_sem.at[1]),
        pltpu.make_async_copy(k_ref, kk.at[core], local_sem.at[2]),
        pltpu.make_async_copy(v_ref, vv.at[core], local_sem.at[3]),
    ]
    for load in loads:
        load.start()
    for n in range(chunks):
        part = pl.ds(n * chunk, chunk)
        pltpu.make_async_copy(p_ref.at[0, part], pb.at[part], p_sem.at[n]).start()

    barrier = pltpu.get_barrier_semaphore()

    def peer(offset):
        other = lax.rem(me + offset, group)
        return {"query": other % heads, "context": 2 * z + other // heads}

    for offset in range(1, group):
        pl.semaphore_signal(barrier, inc=1, device_id=peer(offset), device_id_type=MESH)
    for step in range(1, chips):
        @pl.when(z + step < chips)
        def _():
            pl.semaphore_signal(
                barrier, inc=1, device_id={"context": spot_at + 2 * step}, device_id_type=MESH
            )
    pl.semaphore_wait(barrier, group - 1 + z)

    def down(step):
        return [
            pltpu.make_async_remote_copy(
                src_ref=src.at[0],
                dst_ref=dst.at[step],
                send_sem=z_send.at[which, step],
                recv_sem=z_recv.at[which, step],
                device_id={"context": spot_at - 2 * step},
                device_id_type=MESH,
            )
            for which, (src, dst) in enumerate(((q_ref, qb), (g_ref, gb)))
        ]

    for step in range(chips - 1, 0, -1):
        @pl.when(z >= step)
        def _():
            for copy in down(step):
                copy.start()

    kv = [
        pltpu.make_async_remote_copy(
            src_ref=src,
            dst_ref=dst.at[core],
            send_sem=kv_send.at[which],
            recv_sem=kv_recv.at[which],
            device_id={"context": spot_at + 1 - 2 * core},
            device_id_type=MESH,
        )
        for which, (src, dst) in enumerate(((k_ref, kk), (v_ref, vv)))
    ]
    for copy in kv:
        copy.start()
    for step in range(1, chips):
        @pl.when(z + step >= chips)
        def _():
            qb[step] = jnp.zeros((rows, width), jnp.bfloat16)
            gb[step] = jnp.zeros((rows, width), jnp.bfloat16)
    for load in loads:
        load.wait()

    q_own, g_own = qb[0], gb[0]
    xt[...] = q_own.astype(jnp.float32).T
    spot = lax.broadcasted_iota(jnp.int32, (8, rows), 0)

    def expand(n, carry):
        part = pl.ds(pl.multiple_of(n * chunk, chunk), chunk)
        pltpu.make_async_copy(p_ref.at[0, part], pb.at[part], p_sem.at[n]).wait()
        fb[part, :] = dot(pb[part, :], g_own, NT)
        return carry

    lax.fori_loop(0, chunks, expand, 0)
    total = jnp.zeros((width, rows), jnp.float32)
    cross = []
    for tile in range(width // 8):
        length = width - 8 * tile

        def one(r, total, tile=tile, length=length):
            i = 8 * tile + r
            begin = i * width - (i * (i - 1)) // 2 - r
            feat = fb[pl.ds(begin, length), :]
            weight = jnp.where(spot < r, 0.0, jnp.where(spot == r, np.float32(np.sqrt(0.5)), 1.0))
            head = feat[:8] * weight
            feat = jnp.concatenate([head, feat[8:]], axis=0) if length > 8 else head
            row = xt[pl.ds(i, 1), :]
            x_tile = xt[8 * tile:, :]
            red[i] = jnp.sum((feat * x_tile).reshape(length // 8, 8, rows), axis=0)
            return total + feat * row

        total = lax.fori_loop(0, 8, one, total, unroll=2)
        cross.append(total[:8])
        total = total[8:]
    cross_t = jnp.concatenate(cross, axis=0) + jnp.sum(red[...], axis=1)
    cross_q = (scale * np.sqrt(2.0)) * cross_t.T

    for copy in kv:
        copy.wait()
    keys = kk[...].reshape(2 * rows, width)
    vals = vv[...].reshape(2 * rows, width)

    def weights(q, g):
        score = dot(keys, q, NT)
        return scale * score * score, (2.0 * scale) * score * dot(vals, g, NT)

    own_score = dot(q_own, kk[core], NT)
    own_slope = (2.0 * scale) * own_score * dot(g_own, vv[core], NT)
    own_causal = lax.broadcasted_iota(jnp.int32, (rows, rows), 1) <= lax.broadcasted_iota(
        jnp.int32, (rows, rows), 0
    )
    own_slope = jnp.where(own_causal, own_slope, 0.0).astype(jnp.bfloat16)
    dqb[0] = (dot(own_slope, kk[core], NN) + cross_q).astype(dqb.dtype)
    dq_out = pltpu.make_async_copy(dqb, dq_ref, out_sem.at[0])
    dq_out.start()

    batch = block_batch(chips)
    key_at = lax.broadcasted_iota(jnp.int32, (2 * rows, batch * rows), 0)
    query_at = lax.broadcasted_iota(jnp.int32, (2 * rows, batch * rows), 1)
    causal = key_at <= jnp.where(query_at < rows, query_at + core * rows, 2 * rows)

    def arrive(step):
        @pl.when(z + step < chips)
        def _():
            for copy in down(step):
                copy.wait_recv()

    def key_terms(first, masked):
        part = pl.ds(first, batch)
        q = qb[part].reshape(batch * rows, width)
        g = gb[part].reshape(batch * rows, width)
        attn, slope = weights(q, g)
        if masked:
            attn, slope = jnp.where(causal, attn, 0.0), jnp.where(causal, slope, 0.0)
        return dot(slope.astype(jnp.bfloat16), q, NN), dot(attn.astype(jnp.bfloat16), g, NN)

    for step in range(1, batch):
        arrive(step)
    acc[:, :width], acc[:, width:] = key_terms(0, True)

    def more(n, carry):
        for step in range(batch):
            arrive(n * batch + step)
        to_keys, to_values = key_terms(n * batch, False)
        acc[:, :width] += to_keys
        acc[:, width:] += to_values
        return carry

    if chips > batch:
        lax.fori_loop(1, chips // batch, more, 0)

    sb[...] = acc[...].astype(jnp.bfloat16).reshape(group, share, 2 * width)
    swaps = []
    for offset in range(1, group):
        other = lax.rem(me + offset, group)
        copy = pltpu.make_async_remote_copy(
            src_ref=sb.at[other],
            dst_ref=rb.at[offset],
            send_sem=x_send.at[offset],
            recv_sem=x_recv.at[offset],
            device_id=peer(offset),
            device_id_type=MESH,
        )
        copy.start()
        swaps.append(copy)
    mine = acc[pl.ds(pl.multiple_of(me * share, share), share), :]
    for offset, copy in enumerate(swaps, 1):
        copy.wait_recv()
        mine = mine + rb[offset].astype(jnp.float32)
    dkvb[0] = mine[:, :width].astype(dkvb.dtype)
    dkvb[1] = mine[:, width:].astype(dkvb.dtype)
    dkv_out = pltpu.make_async_copy(dkvb, dkv_ref, out_sem.at[1])
    dkv_out.start()

    for copy in swaps:
        copy.wait_send()
    for step in range(1, chips):
        @pl.when(z >= step)
        def _():
            for copy in down(step):
                copy.wait_send()
    dq_out.wait()
    dkv_out.wait()


def body(queries, keys, values, out_grad, prefix_states):
    heads = lax.axis_size("query")
    chips = lax.axis_size("context") // 2
    group = 2 * heads
    rows, width = keys.shape
    features = prefix_states.shape[1]
    share = rows // heads
    chunks = chunk_count(features)
    whole = jax.ShapeDtypeStruct(queries.shape, jnp.bfloat16)
    half = jax.ShapeDtypeStruct((1, share, width), jnp.bfloat16)
    dma = pltpu.SemaphoreType.DMA
    grad_q, grad_kv = pl.pallas_call(
        kernel,
        out_shape=(whole, jax.ShapeDtypeStruct((2, share, width), jnp.bfloat16)),
        in_specs=[pl.BlockSpec(memory_space=pl.ANY)] * 5,
        out_specs=[pl.BlockSpec(memory_space=pl.ANY)] * 2,
        scratch_shapes=[
            pltpu.VMEM(queries.shape, jnp.bfloat16),
            pltpu.VMEM((2, share, width), jnp.bfloat16),
            pltpu.VMEM((2, rows, width), jnp.bfloat16),
            pltpu.VMEM((2, rows, width), jnp.bfloat16),
            pltpu.VMEM((chips, rows, width), jnp.bfloat16),
            pltpu.VMEM((chips, rows, width), jnp.bfloat16),
            pltpu.VMEM((features, width), jnp.bfloat16),
            pltpu.VMEM((features, rows), jnp.float32),
            pltpu.VMEM((width, rows), jnp.float32),
            pltpu.VMEM((width, 8, rows), jnp.float32),
            pltpu.VMEM((2 * rows, 2 * width), jnp.float32),
            pltpu.VMEM((group, share, 2 * width), jnp.bfloat16),
            pltpu.VMEM((group, share, 2 * width), jnp.bfloat16),
            dma((2,)),
            dma((4,)),
            dma((chunks,)),
            dma((2,)),
            dma((2,)),
            dma((2, chips)),
            dma((2, chips)),
            dma((group,)),
            dma((group,)),
        ],
        compiler_params=pltpu.CompilerParams(
            collective_id=0, has_side_effects=True, vmem_limit_bytes=55168 * 1024
        ),
        cost_estimate=pl.CostEstimate(
            flops=2 * features * width * rows, bytes_accessed=2 * features * width, transcendentals=0
        ),
        name="power_backward",
    )(queries, keys, values, out_grad, prefix_states)
    return pl.pallas_call(
        place,
        out_shape=(whole, half, half),
        in_specs=[pl.BlockSpec(memory_space=pl.ANY)] * 2,
        out_specs=[pl.BlockSpec(memory_space=pl.ANY)] * 3,
        scratch_shapes=[dma((3,))],
        compiler_params=pltpu.CompilerParams(vmem_limit_bytes=55168 * 1024),
        name="place_results",
    )(grad_q, grad_kv)


def solution(mesh):
    return jax.shard_map(
        body,
        mesh=mesh,
        in_specs=(
            P("query", "context", None),
            P("context", None),
            P("context", None),
            P("query", "context", None),
            P("context", None, None),
        ),
        out_specs=(
            P("query", "context", None),
            P("context", "query", None),
            P("context", "query", None),
        ),
        check_vma=False,
    )
```

```python
import functools

import jax
import jax.numpy as jnp
import numpy as np
from jax import lax
from jax.experimental import pallas as pl
from jax.experimental.pallas import tpu as pltpu
from jax.sharding import PartitionSpec as P

MESH = pl.DeviceIdType.MESH
NT = (((1,), (1,)), ((), ()))
NN = (((1,), (0,)), ((), ()))


def dot(a, b, dims):
    return lax.dot_general(a, b, dims, preferred_element_type=jnp.float32)


def chunk_count(features, most=4):
    for count in range(most, 0, -1):
        if features % (16 * count) == 0:
            return count
    return 1


def place(dq_in, dkv_in, dq_out, dk_out, dv_out, sems):
    copies = [
        pltpu.make_async_copy(src, dst, sems.at[n])
        for n, (src, dst) in enumerate(
            ((dq_in, dq_out), (dkv_in.at[0], dk_out.at[0]), (dkv_in.at[1], dv_out.at[0]))
        )
    ]
    for copy in copies:
        copy.start()
    for copy in copies:
        copy.wait()


def kernel(
    q_ref, k_ref, v_ref, g_ref, p_ref, dq_ref, dkv_ref,
    dqb, dkvb, kk, vv, qb, gb, pb, fb, xt, red, acc, sb, rb,
    out_sem, local_sem, p_sem, kv_send, kv_recv, z_send, z_recv, x_send, x_recv,
):
    heads = lax.axis_size("query")
    chips = lax.axis_size("context") // 2
    group = 2 * heads
    h = lax.axis_index("query")
    spot_at = lax.axis_index("context")
    z, core = spot_at // 2, spot_at % 2
    me = core * heads + h
    rows, width = q_ref.shape[1], q_ref.shape[2]
    features = p_ref.shape[1]
    scale = 1.0 / (width * rows)
    share = rows // heads
    chunks = chunk_count(features)
    chunk = features // chunks

    barrier = pltpu.get_barrier_semaphore()

    def peer(offset):
        other = lax.rem(me + offset, group)
        return {"query": other % heads, "context": 2 * z + other // heads}

    for offset in range(1, group):
        pl.semaphore_signal(barrier, inc=1, device_id=peer(offset), device_id_type=MESH)
    for step in range(1, chips):
        @pl.when(z + step < chips)
        def _():
            pl.semaphore_signal(
                barrier, inc=1, device_id={"context": spot_at + 2 * step}, device_id_type=MESH
            )
    loads = [
        pltpu.make_async_copy(q_ref.at[0], qb.at[0], local_sem.at[0]),
        pltpu.make_async_copy(g_ref.at[0], gb.at[0], local_sem.at[1]),
        pltpu.make_async_copy(k_ref, kk.at[core], local_sem.at[2]),
        pltpu.make_async_copy(v_ref, vv.at[core], local_sem.at[3]),
    ]
    for load in loads:
        load.start()
    for n in range(chunks):
        part = pl.ds(n * chunk, chunk)
        pltpu.make_async_copy(p_ref.at[0, part], pb.at[part], p_sem.at[n]).start()

    pl.semaphore_wait(barrier, group - 1 + z)

    def down(step):
        return [
            pltpu.make_async_remote_copy(
                src_ref=src.at[0],
                dst_ref=dst.at[step],
                send_sem=z_send.at[which, step],
                recv_sem=z_recv.at[which, step],
                device_id={"context": spot_at - 2 * step},
                device_id_type=MESH,
            )
            for which, (src, dst) in enumerate(((q_ref, qb), (g_ref, gb)))
        ]

    for step in range(chips - 1, 0, -1):
        @pl.when(z >= step)
        def _():
            for copy in down(step):
                copy.start()

    kv = [
        pltpu.make_async_remote_copy(
            src_ref=src,
            dst_ref=dst.at[core],
            send_sem=kv_send.at[which],
            recv_sem=kv_recv.at[which],
            device_id={"context": spot_at + 1 - 2 * core},
            device_id_type=MESH,
        )
        for which, (src, dst) in enumerate(((k_ref, kk), (v_ref, vv)))
    ]
    for copy in kv:
        copy.start()
    for load in loads:
        load.wait()

    q_own, g_own = qb[0], gb[0]
    xt[...] = q_own.astype(jnp.float32).T
    spot = lax.broadcasted_iota(jnp.int32, (8, rows), 0)

    def expand(n, carry):
        part = pl.ds(pl.multiple_of(n * chunk, chunk), chunk)
        pltpu.make_async_copy(p_ref.at[0, part], pb.at[part], p_sem.at[n]).wait()
        fb[part, :] = dot(pb[part, :], g_own, NT)
        return carry

    lax.fori_loop(0, chunks, expand, 0)
    total = jnp.zeros((width, rows), jnp.float32)
    cross = []
    for tile in range(width // 8):
        length = width - 8 * tile

        def one(r, total, tile=tile, length=length):
            i = 8 * tile + r
            begin = i * width - (i * (i - 1)) // 2 - r
            feat = fb[pl.ds(begin, length), :]
            weight = jnp.where(spot < r, 0.0, jnp.where(spot == r, np.float32(np.sqrt(0.5)), 1.0))
            head = feat[:8] * weight
            feat = jnp.concatenate([head, feat[8:]], axis=0) if length > 8 else head
            row = xt[pl.ds(i, 1), :]
            x_tile = xt[8 * tile:, :]
            red[i] = jnp.sum((feat * x_tile).reshape(length // 8, 8, rows), axis=0)
            return total + feat * row

        total = lax.fori_loop(0, 8, one, total, unroll=2)
        cross.append(total[:8])
        total = total[8:]
    cross_t = jnp.concatenate(cross, axis=0) + jnp.sum(red[...], axis=1)
    cross_q = (scale * np.sqrt(2.0)) * cross_t.T

    for copy in kv:
        copy.wait()
    keys = kk[...].reshape(2 * rows, width)
    vals = vv[...].reshape(2 * rows, width)

    def weights(q, g):
        score = dot(keys, q, NT)
        return scale * score * score, (2.0 * scale) * score * dot(vals, g, NT)

    attn, slope = weights(q_own, g_own)
    key_at = lax.broadcasted_iota(jnp.int32, (2 * rows, rows), 0)
    query_at = lax.broadcasted_iota(jnp.int32, (2 * rows, rows), 1) + core * rows
    causal = key_at <= query_at
    attn = jnp.where(causal, attn, 0.0).astype(jnp.bfloat16)
    slope = jnp.where(causal, slope, 0.0).astype(jnp.bfloat16)
    acc[:, :width] = dot(slope, q_own, NN)
    acc[:, width:] = dot(attn, g_own, NN)
    own_score = dot(q_own, kk[core], NT)
    own_slope = (2.0 * scale) * own_score * dot(g_own, vv[core], NT)
    own_causal = lax.broadcasted_iota(jnp.int32, (rows, rows), 1) <= lax.broadcasted_iota(
        jnp.int32, (rows, rows), 0
    )
    own_slope = jnp.where(own_causal, own_slope, 0.0).astype(jnp.bfloat16)
    dqb[0] = (dot(own_slope, kk[core], NN) + cross_q).astype(dqb.dtype)
    dq_out = pltpu.make_async_copy(dqb, dq_ref, out_sem.at[0])
    dq_out.start()

    def later(step, carry):
        for copy in down(step):
            copy.wait_recv()
        q, g = qb[step], gb[step]
        attn, slope = weights(q, g)
        acc[:, :width] += dot(slope.astype(jnp.bfloat16), q, NN)
        acc[:, width:] += dot(attn.astype(jnp.bfloat16), g, NN)
        return carry

    lax.fori_loop(1, chips - z, later, 0)

    sb[...] = acc[...].astype(jnp.bfloat16).reshape(group, share, 2 * width)
    swaps = []
    for offset in range(1, group):
        other = lax.rem(me + offset, group)
        copy = pltpu.make_async_remote_copy(
            src_ref=sb.at[other],
            dst_ref=rb.at[offset],
            send_sem=x_send.at[offset],
            recv_sem=x_recv.at[offset],
            device_id=peer(offset),
            device_id_type=MESH,
        )
        copy.start()
        swaps.append(copy)
    mine = acc[pl.ds(pl.multiple_of(me * share, share), share), :]
    for offset, copy in enumerate(swaps, 1):
        copy.wait_recv()
        mine = mine + rb[offset].astype(jnp.float32)
    dkvb[0] = mine[:, :width].astype(dkvb.dtype)
    dkvb[1] = mine[:, width:].astype(dkvb.dtype)
    dkv_out = pltpu.make_async_copy(dkvb, dkv_ref, out_sem.at[1])
    dkv_out.start()

    for copy in swaps:
        copy.wait_send()
    for step in range(1, chips):
        @pl.when(z >= step)
        def _():
            for copy in down(step):
                copy.wait_send()
    dq_out.wait()
    dkv_out.wait()


def body(queries, keys, values, out_grad, prefix_states):
    heads = lax.axis_size("query")
    chips = lax.axis_size("context") // 2
    group = 2 * heads
    rows, width = keys.shape
    features = prefix_states.shape[1]
    share = rows // heads
    chunks = chunk_count(features)
    whole = jax.ShapeDtypeStruct(queries.shape, jnp.bfloat16)
    half = jax.ShapeDtypeStruct((1, share, width), jnp.bfloat16)
    dma = pltpu.SemaphoreType.DMA
    grad_q, grad_kv = pl.pallas_call(
        kernel,
        out_shape=(whole, jax.ShapeDtypeStruct((2, share, width), jnp.bfloat16)),
        in_specs=[pl.BlockSpec(memory_space=pl.ANY)] * 5,
        out_specs=[pl.BlockSpec(memory_space=pl.ANY)] * 2,
        scratch_shapes=[
            pltpu.VMEM(queries.shape, jnp.bfloat16),
            pltpu.VMEM((2, share, width), jnp.bfloat16),
            pltpu.VMEM((2, rows, width), jnp.bfloat16),
            pltpu.VMEM((2, rows, width), jnp.bfloat16),
            pltpu.VMEM((chips, rows, width), jnp.bfloat16),
            pltpu.VMEM((chips, rows, width), jnp.bfloat16),
            pltpu.VMEM((features, width), jnp.bfloat16),
            pltpu.VMEM((features, rows), jnp.float32),
            pltpu.VMEM((width, rows), jnp.float32),
            pltpu.VMEM((width, 8, rows), jnp.float32),
            pltpu.VMEM((2 * rows, 2 * width), jnp.float32),
            pltpu.VMEM((group, share, 2 * width), jnp.bfloat16),
            pltpu.VMEM((group, share, 2 * width), jnp.bfloat16),
            dma((2,)),
            dma((4,)),
            dma((chunks,)),
            dma((2,)),
            dma((2,)),
            dma((2, chips)),
            dma((2, chips)),
            dma((group,)),
            dma((group,)),
        ],
        compiler_params=pltpu.CompilerParams(
            collective_id=0, has_side_effects=True, vmem_limit_bytes=55168 * 1024
        ),
        cost_estimate=pl.CostEstimate(
            flops=2 * features * width * rows, bytes_accessed=2 * features * width, transcendentals=0
        ),
        name="power_backward",
    )(queries, keys, values, out_grad, prefix_states)
    return pl.pallas_call(
        place,
        out_shape=(whole, half, half),
        in_specs=[pl.BlockSpec(memory_space=pl.ANY)] * 2,
        out_specs=[pl.BlockSpec(memory_space=pl.ANY)] * 3,
        scratch_shapes=[dma((3,))],
        compiler_params=pltpu.CompilerParams(vmem_limit_bytes=55168 * 1024),
        name="place_results",
    )(grad_q, grad_kv)


def solution(mesh):
    return jax.shard_map(
        body,
        mesh=mesh,
        in_specs=(
            P("query", "context", None),
            P("context", None),
            P("context", None),
            P("query", "context", None),
            P("context", None, None),
        ),
        out_specs=(
            P("query", "context", None),
            P("context", "query", None),
            P("context", "query", None),
        ),
        check_vma=False,
    )
```

```python
import functools

import jax
import jax.numpy as jnp
import numpy as np
from jax import lax
from jax.experimental import pallas as pl
from jax.experimental.pallas import tpu as pltpu
from jax.sharding import PartitionSpec as P

MESH = pl.DeviceIdType.MESH
NT = (((1,), (1,)), ((), ()))
NN = (((1,), (0,)), ((), ()))


def dot(a, b, dims):
    return lax.dot_general(a, b, dims, preferred_element_type=jnp.float32)


def chunk_count(features, most=4):
    for count in range(most, 0, -1):
        if features % (16 * count) == 0:
            return count
    return 1


def block_batch(chips, most=4):
    return max(size for size in range(1, most + 1) if chips % size == 0)


def place(dq_in, dkv_in, dq_out, dk_out, dv_out, sems):
    copies = [
        pltpu.make_async_copy(src, dst, sems.at[n])
        for n, (src, dst) in enumerate(
            ((dq_in, dq_out), (dkv_in.at[0], dk_out.at[0]), (dkv_in.at[1], dv_out.at[0]))
        )
    ]
    for copy in copies:
        copy.start()
    for copy in copies:
        copy.wait()


def kernel(
    q_ref, k_ref, v_ref, g_ref, p_ref, dq_ref, dkv_ref,
    dqb, dkvb, kk, vv, qb, gb, pb, fb, xt, red, acc, sb, rb,
    out_sem, local_sem, p_sem, kv_send, kv_recv, z_send, z_recv, x_send, x_recv,
):
    heads = lax.axis_size("query")
    chips = lax.axis_size("context") // 2
    group = 2 * heads
    h = lax.axis_index("query")
    spot_at = lax.axis_index("context")
    z, core = spot_at // 2, spot_at % 2
    me = core * heads + h
    rows, width = q_ref.shape[1], q_ref.shape[2]
    features = p_ref.shape[1]
    scale = 1.0 / (width * rows)
    share = rows // heads
    chunks = chunk_count(features)
    chunk = features // chunks

    barrier = pltpu.get_barrier_semaphore()

    def peer(offset):
        other = lax.rem(me + offset, group)
        return {"query": other % heads, "context": 2 * z + other // heads}

    for offset in range(1, group):
        pl.semaphore_signal(barrier, inc=1, device_id=peer(offset), device_id_type=MESH)
    for step in range(1, chips):
        @pl.when(z + step < chips)
        def _():
            pl.semaphore_signal(
                barrier, inc=1, device_id={"context": spot_at + 2 * step}, device_id_type=MESH
            )
    loads = [
        pltpu.make_async_copy(q_ref.at[0], qb.at[0], local_sem.at[0]),
        pltpu.make_async_copy(g_ref.at[0], gb.at[0], local_sem.at[1]),
        pltpu.make_async_copy(k_ref, kk.at[core], local_sem.at[2]),
        pltpu.make_async_copy(v_ref, vv.at[core], local_sem.at[3]),
    ]
    for load in loads:
        load.start()
    for n in range(chunks):
        part = pl.ds(n * chunk, chunk)
        pltpu.make_async_copy(p_ref.at[0, part], pb.at[part], p_sem.at[n]).start()

    pl.semaphore_wait(barrier, group - 1 + z)

    def down(step):
        return [
            pltpu.make_async_remote_copy(
                src_ref=src.at[0],
                dst_ref=dst.at[step],
                send_sem=z_send.at[which, step],
                recv_sem=z_recv.at[which, step],
                device_id={"context": spot_at - 2 * step},
                device_id_type=MESH,
            )
            for which, (src, dst) in enumerate(((q_ref, qb), (g_ref, gb)))
        ]

    def send_to(chip):
        @pl.when(z > chip)
        def _():
            for copy in down(z - chip):
                copy.start()

    send_to(0)

    kv = [
        pltpu.make_async_remote_copy(
            src_ref=src,
            dst_ref=dst.at[core],
            send_sem=kv_send.at[which],
            recv_sem=kv_recv.at[which],
            device_id={"context": spot_at + 1 - 2 * core},
            device_id_type=MESH,
        )
        for which, (src, dst) in enumerate(((k_ref, kk), (v_ref, vv)))
    ]
    for copy in kv:
        copy.start()
    for step in range(1, chips):
        @pl.when(z + step >= chips)
        def _():
            qb[step] = jnp.zeros((rows, width), jnp.bfloat16)
            gb[step] = jnp.zeros((rows, width), jnp.bfloat16)
    for load in loads:
        load.wait()

    q_own, g_own = qb[0], gb[0]
    xt[...] = q_own.astype(jnp.float32).T
    spot = lax.broadcasted_iota(jnp.int32, (8, rows), 0)

    def expand(n, carry):
        part = pl.ds(pl.multiple_of(n * chunk, chunk), chunk)
        pltpu.make_async_copy(p_ref.at[0, part], pb.at[part], p_sem.at[n]).wait()
        fb[part, :] = dot(pb[part, :], g_own, NT)
        return carry

    lax.fori_loop(0, chunks, expand, 0)
    send_to(1)
    total = jnp.zeros((width, rows), jnp.float32)
    cross = []
    for tile in range(width // 8):
        length = width - 8 * tile
        if tile == 3:

            def send_rest(chip, carry):
                for copy in down(z - chip):
                    copy.start()
                return carry

            lax.fori_loop(2, z, send_rest, 0)

        def one(r, total, tile=tile, length=length):
            i = 8 * tile + r
            begin = i * width - (i * (i - 1)) // 2 - r
            feat = fb[pl.ds(begin, length), :]
            weight = jnp.where(spot < r, 0.0, jnp.where(spot == r, np.float32(np.sqrt(0.5)), 1.0))
            head = feat[:8] * weight
            feat = jnp.concatenate([head, feat[8:]], axis=0) if length > 8 else head
            row = xt[pl.ds(i, 1), :]
            x_tile = xt[8 * tile:, :]
            red[i] = jnp.sum((feat * x_tile).reshape(length // 8, 8, rows), axis=0)
            return total + feat * row

        total = lax.fori_loop(0, 8, one, total, unroll=2)
        cross.append(total[:8])
        total = total[8:]
    cross_t = jnp.concatenate(cross, axis=0) + jnp.sum(red[...], axis=1)
    cross_q = (scale * np.sqrt(2.0)) * cross_t.T

    for copy in kv:
        copy.wait()
    keys = kk[...].reshape(2 * rows, width)
    vals = vv[...].reshape(2 * rows, width)

    def weights(q, g):
        score = dot(keys, q, NT)
        return scale * score * score, (2.0 * scale) * score * dot(vals, g, NT)

    own_score = dot(q_own, kk[core], NT)
    own_slope = (2.0 * scale) * own_score * dot(g_own, vv[core], NT)
    own_causal = lax.broadcasted_iota(jnp.int32, (rows, rows), 1) <= lax.broadcasted_iota(
        jnp.int32, (rows, rows), 0
    )
    own_slope = jnp.where(own_causal, own_slope, 0.0).astype(jnp.bfloat16)
    dqb[0] = (dot(own_slope, kk[core], NN) + cross_q).astype(dqb.dtype)
    dq_out = pltpu.make_async_copy(dqb, dq_ref, out_sem.at[0])
    dq_out.start()

    batch = block_batch(chips)
    key_at = lax.broadcasted_iota(jnp.int32, (2 * rows, batch * rows), 0)
    query_at = lax.broadcasted_iota(jnp.int32, (2 * rows, batch * rows), 1)
    causal = key_at <= jnp.where(query_at < rows, query_at + core * rows, 2 * rows)

    def arrive(step):
        @pl.when(z + step < chips)
        def _():
            for copy in down(step):
                copy.wait_recv()

    def key_terms(first, masked):
        part = pl.ds(first, batch)
        q = qb[part].reshape(batch * rows, width)
        g = gb[part].reshape(batch * rows, width)
        attn, slope = weights(q, g)
        if masked:
            attn, slope = jnp.where(causal, attn, 0.0), jnp.where(causal, slope, 0.0)
        return dot(slope.astype(jnp.bfloat16), q, NN), dot(attn.astype(jnp.bfloat16), g, NN)

    for step in range(1, batch):
        arrive(step)
    acc[:, :width], acc[:, width:] = key_terms(0, True)

    def more(n, carry):
        for step in range(batch):
            arrive(n * batch + step)
        to_keys, to_values = key_terms(n * batch, False)
        acc[:, :width] += to_keys
        acc[:, width:] += to_values
        return carry

    if chips > batch:
        lax.fori_loop(1, chips // batch, more, 0)

    sb[...] = acc[...].astype(jnp.bfloat16).reshape(group, share, 2 * width)
    swaps = []
    for offset in range(1, group):
        other = lax.rem(me + offset, group)
        copy = pltpu.make_async_remote_copy(
            src_ref=sb.at[other],
            dst_ref=rb.at[offset],
            send_sem=x_send.at[offset],
            recv_sem=x_recv.at[offset],
            device_id=peer(offset),
            device_id_type=MESH,
        )
        copy.start()
        swaps.append(copy)
    mine = acc[pl.ds(pl.multiple_of(me * share, share), share), :]
    for offset, copy in enumerate(swaps, 1):
        copy.wait_recv()
        mine = mine + rb[offset].astype(jnp.float32)
    dkvb[0] = mine[:, :width].astype(dkvb.dtype)
    dkvb[1] = mine[:, width:].astype(dkvb.dtype)
    dkv_out = pltpu.make_async_copy(dkvb, dkv_ref, out_sem.at[1])
    dkv_out.start()

    for copy in swaps:
        copy.wait_send()
    for step in range(1, chips):
        @pl.when(z >= step)
        def _():
            for copy in down(step):
                copy.wait_send()
    dq_out.wait()
    dkv_out.wait()


def body(queries, keys, values, out_grad, prefix_states):
    heads = lax.axis_size("query")
    chips = lax.axis_size("context") // 2
    group = 2 * heads
    rows, width = keys.shape
    features = prefix_states.shape[1]
    share = rows // heads
    chunks = chunk_count(features)
    whole = jax.ShapeDtypeStruct(queries.shape, jnp.bfloat16)
    half = jax.ShapeDtypeStruct((1, share, width), jnp.bfloat16)
    dma = pltpu.SemaphoreType.DMA
    grad_q, grad_kv = pl.pallas_call(
        kernel,
        out_shape=(whole, jax.ShapeDtypeStruct((2, share, width), jnp.bfloat16)),
        in_specs=[pl.BlockSpec(memory_space=pl.ANY)] * 5,
        out_specs=[pl.BlockSpec(memory_space=pl.ANY)] * 2,
        scratch_shapes=[
            pltpu.VMEM(queries.shape, jnp.bfloat16),
            pltpu.VMEM((2, share, width), jnp.bfloat16),
            pltpu.VMEM((2, rows, width), jnp.bfloat16),
            pltpu.VMEM((2, rows, width), jnp.bfloat16),
            pltpu.VMEM((chips, rows, width), jnp.bfloat16),
            pltpu.VMEM((chips, rows, width), jnp.bfloat16),
            pltpu.VMEM((features, width), jnp.bfloat16),
            pltpu.VMEM((features, rows), jnp.float32),
            pltpu.VMEM((width, rows), jnp.float32),
            pltpu.VMEM((width, 8, rows), jnp.float32),
            pltpu.VMEM((2 * rows, 2 * width), jnp.float32),
            pltpu.VMEM((group, share, 2 * width), jnp.bfloat16),
            pltpu.VMEM((group, share, 2 * width), jnp.bfloat16),
            dma((2,)),
            dma((4,)),
            dma((chunks,)),
            dma((2,)),
            dma((2,)),
            dma((2, chips)),
            dma((2, chips)),
            dma((group,)),
            dma((group,)),
        ],
        compiler_params=pltpu.CompilerParams(
            collective_id=0, has_side_effects=True, vmem_limit_bytes=55168 * 1024
        ),
        cost_estimate=pl.CostEstimate(
            flops=2 * features * width * rows, bytes_accessed=2 * features * width, transcendentals=0
        ),
        name="power_backward",
    )(queries, keys, values, out_grad, prefix_states)
    return pl.pallas_call(
        place,
        out_shape=(whole, half, half),
        in_specs=[pl.BlockSpec(memory_space=pl.ANY)] * 2,
        out_specs=[pl.BlockSpec(memory_space=pl.ANY)] * 3,
        scratch_shapes=[dma((3,))],
        compiler_params=pltpu.CompilerParams(vmem_limit_bytes=55168 * 1024),
        name="place_results",
    )(grad_q, grad_kv)


def solution(mesh):
    return jax.shard_map(
        body,
        mesh=mesh,
        in_specs=(
            P("query", "context", None),
            P("context", None),
            P("context", None),
            P("query", "context", None),
            P("context", None, None),
        ),
        out_specs=(
            P("query", "context", None),
            P("context", "query", None),
            P("context", "query", None),
        ),
        check_vma=False,
    )
```

```python
import functools

import jax
import jax.numpy as jnp
import numpy as np
from jax import lax
from jax.experimental import pallas as pl
from jax.experimental.pallas import tpu as pltpu
from jax.sharding import PartitionSpec as P

MESH = pl.DeviceIdType.MESH
NT = (((1,), (1,)), ((), ()))
NN = (((1,), (0,)), ((), ()))


def dot(a, b, dims):
    return lax.dot_general(a, b, dims, preferred_element_type=jnp.float32)


def chunk_count(features, most=4):
    for count in range(most, 0, -1):
        if features % (16 * count) == 0:
            return count
    return 1


def later_batches(chips, most=3):
    batch = max(1, min(most, chips - 1))
    return batch, -(-(chips - 1) // batch)


def place(dq_in, dkv_in, dq_out, dk_out, dv_out, sems):
    copies = [
        pltpu.make_async_copy(src, dst, sems.at[n])
        for n, (src, dst) in enumerate(
            ((dq_in, dq_out), (dkv_in.at[0], dk_out.at[0]), (dkv_in.at[1], dv_out.at[0]))
        )
    ]
    for copy in copies:
        copy.start()
    for copy in copies:
        copy.wait()


def kernel(
    q_ref, k_ref, v_ref, g_ref, p_ref, dq_ref, dkv_ref,
    dqb, dkvb, kk, vv, qb, gb, pb, fb, xt, red, acc, sb, rb,
    out_sem, local_sem, p_sem, kv_send, kv_recv, z_send, z_recv, x_send, x_recv,
):
    heads = lax.axis_size("query")
    chips = lax.axis_size("context") // 2
    group = 2 * heads
    h = lax.axis_index("query")
    spot_at = lax.axis_index("context")
    z, core = spot_at // 2, spot_at % 2
    me = core * heads + h
    rows, width = q_ref.shape[1], q_ref.shape[2]
    features = p_ref.shape[1]
    scale = 1.0 / (width * rows)
    share = rows // heads
    chunks = chunk_count(features)
    chunk = features // chunks

    barrier = pltpu.get_barrier_semaphore()

    def peer(offset):
        other = lax.rem(me + offset, group)
        return {"query": other % heads, "context": 2 * z + other // heads}

    for offset in range(1, group):
        pl.semaphore_signal(barrier, inc=1, device_id=peer(offset), device_id_type=MESH)
    for step in range(1, chips):
        @pl.when(z + step < chips)
        def _():
            pl.semaphore_signal(
                barrier, inc=1, device_id={"context": spot_at + 2 * step}, device_id_type=MESH
            )
    loads = [
        pltpu.make_async_copy(q_ref.at[0], qb.at[0], local_sem.at[0]),
        pltpu.make_async_copy(g_ref.at[0], gb.at[0], local_sem.at[1]),
        pltpu.make_async_copy(k_ref, kk.at[core], local_sem.at[2]),
        pltpu.make_async_copy(v_ref, vv.at[core], local_sem.at[3]),
    ]
    for load in loads:
        load.start()
    for n in range(chunks):
        part = pl.ds(n * chunk, chunk)
        pltpu.make_async_copy(p_ref.at[0, part], pb.at[part], p_sem.at[n]).start()

    pl.semaphore_wait(barrier, group - 1 + z)

    def down(step):
        return [
            pltpu.make_async_remote_copy(
                src_ref=src.at[0],
                dst_ref=dst.at[step],
                send_sem=z_send.at[which, step],
                recv_sem=z_recv.at[which, step],
                device_id={"context": spot_at - 2 * step},
                device_id_type=MESH,
            )
            for which, (src, dst) in enumerate(((q_ref, qb), (g_ref, gb)))
        ]

    def send_to(chip):
        @pl.when(z > chip)
        def _():
            for copy in down(z - chip):
                copy.start()

    send_to(0)

    kv = [
        pltpu.make_async_remote_copy(
            src_ref=src,
            dst_ref=dst.at[core],
            send_sem=kv_send.at[which],
            recv_sem=kv_recv.at[which],
            device_id={"context": spot_at + 1 - 2 * core},
            device_id_type=MESH,
        )
        for which, (src, dst) in enumerate(((k_ref, kk), (v_ref, vv)))
    ]
    for copy in kv:
        copy.start()
    for step in range(1, qb.shape[0]):
        @pl.when(z + step >= chips)
        def _():
            qb[step] = jnp.zeros((rows, width), jnp.bfloat16)
            gb[step] = jnp.zeros((rows, width), jnp.bfloat16)
    for load in loads:
        load.wait()

    q_own, g_own = qb[0], gb[0]
    xt[...] = q_own.astype(jnp.float32).T
    spot = lax.broadcasted_iota(jnp.int32, (8, rows), 0)

    def expand(n, carry):
        part = pl.ds(pl.multiple_of(n * chunk, chunk), chunk)
        pltpu.make_async_copy(p_ref.at[0, part], pb.at[part], p_sem.at[n]).wait()
        fb[part, :] = dot(pb[part, :], g_own, NT)
        return carry

    lax.fori_loop(0, chunks, expand, 0)
    send_to(1)
    total = jnp.zeros((width, rows), jnp.float32)
    cross = []
    for tile in range(width // 8):
        length = width - 8 * tile
        if tile == 3:

            def send_rest(chip, carry):
                for copy in down(z - chip):
                    copy.start()
                return carry

            lax.fori_loop(2, z, send_rest, 0)

        def one(r, total, tile=tile, length=length):
            i = 8 * tile + r
            begin = i * width - (i * (i - 1)) // 2 - r
            feat = fb[pl.ds(begin, length), :]
            weight = jnp.where(spot < r, 0.0, jnp.where(spot == r, np.float32(np.sqrt(0.5)), 1.0))
            head = feat[:8] * weight
            feat = jnp.concatenate([head, feat[8:]], axis=0) if length > 8 else head
            row = xt[pl.ds(i, 1), :]
            x_tile = xt[8 * tile:, :]
            red[i] = jnp.sum((feat * x_tile).reshape(length // 8, 8, rows), axis=0)
            return total + feat * row

        total = lax.fori_loop(0, 8, one, total, unroll=2)
        cross.append(total[:8])
        total = total[8:]
    cross_t = jnp.concatenate(cross, axis=0) + jnp.sum(red[...], axis=1)
    cross_q = (scale * np.sqrt(2.0)) * cross_t.T

    for copy in kv:
        copy.wait()
    keys = kk[...].reshape(2 * rows, width)
    vals = vv[...].reshape(2 * rows, width)

    def weights(q, g):
        score = dot(keys, q, NT)
        return scale * score * score, (2.0 * scale) * score * dot(vals, g, NT)

    attn, slope = weights(q_own, g_own)
    key_at = lax.broadcasted_iota(jnp.int32, (2 * rows, rows), 0)
    query_at = lax.broadcasted_iota(jnp.int32, (2 * rows, rows), 1) + core * rows
    causal = key_at <= query_at
    attn = jnp.where(causal, attn, 0.0).astype(jnp.bfloat16)
    slope = jnp.where(causal, slope, 0.0).astype(jnp.bfloat16)
    acc[:, :width] = dot(slope, q_own, NN)
    acc[:, width:] = dot(attn, g_own, NN)
    own_score = dot(q_own, kk[core], NT)
    own_slope = (2.0 * scale) * own_score * dot(g_own, vv[core], NT)
    own_causal = lax.broadcasted_iota(jnp.int32, (rows, rows), 1) <= lax.broadcasted_iota(
        jnp.int32, (rows, rows), 0
    )
    own_slope = jnp.where(own_causal, own_slope, 0.0).astype(jnp.bfloat16)
    dqb[0] = (dot(own_slope, kk[core], NN) + cross_q).astype(dqb.dtype)
    dq_out = pltpu.make_async_copy(dqb, dq_ref, out_sem.at[0])
    dq_out.start()

    batch, batches = later_batches(chips)

    def later(n, carry):
        first = 1 + n * batch
        for extra in range(batch):
            @pl.when(z + first + extra < chips)
            def _():
                for copy in down(first + extra):
                    copy.wait_recv()
        part = pl.ds(first, batch)
        q = qb[part].reshape(batch * rows, width)
        g = gb[part].reshape(batch * rows, width)
        attn, slope = weights(q, g)
        acc[:, :width] += dot(slope.astype(jnp.bfloat16), q, NN)
        acc[:, width:] += dot(attn.astype(jnp.bfloat16), g, NN)
        return carry

    if batches == 1:
        later(0, 0)
    else:
        lax.fori_loop(0, batches, later, 0)

    sb[...] = acc[...].astype(jnp.bfloat16).reshape(group, share, 2 * width)
    def swap(dest, offset):
        return pltpu.make_async_remote_copy(
            src_ref=sb.at[dest],
            dst_ref=rb.at[offset],
            send_sem=x_send.at[offset],
            recv_sem=x_recv.at[offset],
            device_id={"query": dest % heads, "context": 2 * z + dest // heads},
            device_id_type=MESH,
        )

    for head in range(heads):
        for half in range(2):
            dest = half * heads + head

            @pl.when(me != dest)
            def _():
                swap(dest, lax.rem(dest - me + group, group)).start()

    swaps = [swap(lax.rem(me + offset, group), offset) for offset in range(1, group)]
    mine = acc[pl.ds(pl.multiple_of(me * share, share), share), :]
    for offset, copy in enumerate(swaps, 1):
        copy.wait_recv()
        mine = mine + rb[offset].astype(jnp.float32)
    dkvb[0] = mine[:, :width].astype(dkvb.dtype)
    dkvb[1] = mine[:, width:].astype(dkvb.dtype)
    dkv_out = pltpu.make_async_copy(dkvb, dkv_ref, out_sem.at[1])
    dkv_out.start()

    for copy in swaps:
        copy.wait_send()
    for step in range(1, chips):
        @pl.when(z >= step)
        def _():
            for copy in down(step):
                copy.wait_send()
    dq_out.wait()
    dkv_out.wait()


def body(queries, keys, values, out_grad, prefix_states):
    heads = lax.axis_size("query")
    chips = lax.axis_size("context") // 2
    group = 2 * heads
    rows, width = keys.shape
    features = prefix_states.shape[1]
    share = rows // heads
    chunks = chunk_count(features)
    batch, batches = later_batches(chips)
    slots = 1 + batch * batches
    whole = jax.ShapeDtypeStruct(queries.shape, jnp.bfloat16)
    half = jax.ShapeDtypeStruct((1, share, width), jnp.bfloat16)
    dma = pltpu.SemaphoreType.DMA
    grad_q, grad_kv = pl.pallas_call(
        kernel,
        out_shape=(whole, jax.ShapeDtypeStruct((2, share, width), jnp.bfloat16)),
        in_specs=[pl.BlockSpec(memory_space=pl.ANY)] * 5,
        out_specs=[pl.BlockSpec(memory_space=pl.ANY)] * 2,
        scratch_shapes=[
            pltpu.VMEM(queries.shape, jnp.bfloat16),
            pltpu.VMEM((2, share, width), jnp.bfloat16),
            pltpu.VMEM((2, rows, width), jnp.bfloat16),
            pltpu.VMEM((2, rows, width), jnp.bfloat16),
            pltpu.VMEM((slots, rows, width), jnp.bfloat16),
            pltpu.VMEM((slots, rows, width), jnp.bfloat16),
            pltpu.VMEM((features, width), jnp.bfloat16),
            pltpu.VMEM((features, rows), jnp.float32),
            pltpu.VMEM((width, rows), jnp.float32),
            pltpu.VMEM((width, 8, rows), jnp.float32),
            pltpu.VMEM((2 * rows, 2 * width), jnp.float32),
            pltpu.VMEM((group, share, 2 * width), jnp.bfloat16),
            pltpu.VMEM((group, share, 2 * width), jnp.bfloat16),
            dma((2,)),
            dma((4,)),
            dma((chunks,)),
            dma((2,)),
            dma((2,)),
            dma((2, chips)),
            dma((2, chips)),
            dma((group,)),
            dma((group,)),
        ],
        compiler_params=pltpu.CompilerParams(
            collective_id=0, has_side_effects=True, vmem_limit_bytes=55168 * 1024
        ),
        cost_estimate=pl.CostEstimate(
            flops=2 * features * width * rows, bytes_accessed=2 * features * width, transcendentals=0
        ),
        name="power_backward",
    )(queries, keys, values, out_grad, prefix_states)
    return pl.pallas_call(
        place,
        out_shape=(whole, half, half),
        in_specs=[pl.BlockSpec(memory_space=pl.ANY)] * 2,
        out_specs=[pl.BlockSpec(memory_space=pl.ANY)] * 3,
        scratch_shapes=[dma((3,))],
        compiler_params=pltpu.CompilerParams(vmem_limit_bytes=55168 * 1024),
        name="place_results",
    )(grad_q, grad_kv)


def solution(mesh):
    return jax.shard_map(
        body,
        mesh=mesh,
        in_specs=(
            P("query", "context", None),
            P("context", None),
            P("context", None),
            P("query", "context", None),
            P("context", None, None),
        ),
        out_specs=(
            P("query", "context", None),
            P("context", "query", None),
            P("context", "query", None),
        ),
        check_vma=False,
    )
```

```python
import functools

import jax
import jax.numpy as jnp
import numpy as np
from jax import lax
from jax.experimental import pallas as pl
from jax.experimental.pallas import tpu as pltpu
from jax.sharding import PartitionSpec as P

MESH = pl.DeviceIdType.MESH
NT = (((1,), (1,)), ((), ()))
NN = (((1,), (0,)), ((), ()))


def dot(a, b, dims):
    return lax.dot_general(a, b, dims, preferred_element_type=jnp.float32)


def chunk_count(features, most=4):
    for count in range(most, 0, -1):
        if features % (16 * count) == 0:
            return count
    return 1


def later_batches(chips, most=3):
    batch = max(1, min(most, chips - 1))
    return batch, -(-(chips - 1) // batch)


def place(dq_in, dkv_in, dq_out, dk_out, dv_out, sems):
    copies = [
        pltpu.make_async_copy(src, dst, sems.at[n])
        for n, (src, dst) in enumerate(
            ((dq_in, dq_out), (dkv_in.at[0], dk_out.at[0]), (dkv_in.at[1], dv_out.at[0]))
        )
    ]
    for copy in copies:
        copy.start()
    for copy in copies:
        copy.wait()


def kernel(
    q_ref, k_ref, v_ref, g_ref, p_ref, dq_ref, dkv_ref,
    dqb, dkvb, kk, vv, qb, gb, pb, fb, xt, red, acc, sb, rb,
    out_sem, local_sem, p_sem, kv_send, kv_recv, z_send, z_recv, x_send, x_recv,
):
    heads = lax.axis_size("query")
    chips = lax.axis_size("context") // 2
    group = 2 * heads
    h = lax.axis_index("query")
    spot_at = lax.axis_index("context")
    z, core = spot_at // 2, spot_at % 2
    me = core * heads + h
    rows, width = q_ref.shape[1], q_ref.shape[2]
    features = p_ref.shape[1]
    scale = 1.0 / (width * rows)
    share = rows // heads
    chunks = chunk_count(features)
    chunk = features // chunks

    barrier = pltpu.get_barrier_semaphore()

    def peer(offset):
        other = lax.rem(me + offset, group)
        return {"query": other % heads, "context": 2 * z + other // heads}

    for offset in range(1, group):
        pl.semaphore_signal(barrier, inc=1, device_id=peer(offset), device_id_type=MESH)
    for step in range(1, chips):
        @pl.when(z + step < chips)
        def _():
            pl.semaphore_signal(
                barrier, inc=1, device_id={"context": spot_at + 2 * step}, device_id_type=MESH
            )
    loads = [
        pltpu.make_async_copy(q_ref.at[0], qb.at[0], local_sem.at[0]),
        pltpu.make_async_copy(g_ref.at[0], gb.at[0], local_sem.at[1]),
        pltpu.make_async_copy(k_ref, kk.at[core], local_sem.at[2]),
        pltpu.make_async_copy(v_ref, vv.at[core], local_sem.at[3]),
    ]
    for load in loads:
        load.start()
    for n in range(chunks):
        part = pl.ds(n * chunk, chunk)
        pltpu.make_async_copy(p_ref.at[0, part], pb.at[part], p_sem.at[n]).start()

    pl.semaphore_wait(barrier, group - 1 + z)

    def down(step):
        return [
            pltpu.make_async_remote_copy(
                src_ref=src.at[0],
                dst_ref=dst.at[step],
                send_sem=z_send.at[which, step],
                recv_sem=z_recv.at[which, step],
                device_id={"context": spot_at - 2 * step},
                device_id_type=MESH,
            )
            for which, (src, dst) in enumerate(((q_ref, qb), (g_ref, gb)))
        ]

    def send_to(chip):
        @pl.when(z > chip)
        def _():
            for copy in down(z - chip):
                copy.start()

    send_to(0)

    kv = [
        pltpu.make_async_remote_copy(
            src_ref=src,
            dst_ref=dst.at[core],
            send_sem=kv_send.at[which],
            recv_sem=kv_recv.at[which],
            device_id={"context": spot_at + 1 - 2 * core},
            device_id_type=MESH,
        )
        for which, (src, dst) in enumerate(((k_ref, kk), (v_ref, vv)))
    ]
    for copy in kv:
        copy.start()
    for step in range(1, qb.shape[0]):
        @pl.when(z + step >= chips)
        def _():
            qb[step] = jnp.zeros((rows, width), jnp.bfloat16)
            gb[step] = jnp.zeros((rows, width), jnp.bfloat16)
    for load in loads:
        load.wait()

    q_own, g_own = qb[0], gb[0]
    xt[...] = q_own.astype(jnp.float32).T
    spot = lax.broadcasted_iota(jnp.int32, (8, rows), 0)

    def expand(n, carry):
        part = pl.ds(pl.multiple_of(n * chunk, chunk), chunk)
        pltpu.make_async_copy(p_ref.at[0, part], pb.at[part], p_sem.at[n]).wait()
        fb[part, :] = dot(pb[part, :], g_own, NT)
        return carry

    lax.fori_loop(0, chunks, expand, 0)
    send_to(1)
    total = jnp.zeros((width, rows), jnp.float32)
    cross = []
    for tile in range(width // 8):
        length = width - 8 * tile
        if tile == 3:

            def send_rest(chip, carry):
                for copy in down(z - chip):
                    copy.start()
                return carry

            lax.fori_loop(2, z, send_rest, 0)

        def one(r, total, tile=tile, length=length):
            i = 8 * tile + r
            begin = i * width - (i * (i - 1)) // 2 - r
            feat = fb[pl.ds(begin, length), :]
            weight = jnp.where(spot < r, 0.0, jnp.where(spot == r, np.float32(np.sqrt(0.5)), 1.0))
            head = feat[:8] * weight
            feat = jnp.concatenate([head, feat[8:]], axis=0) if length > 8 else head
            row = xt[pl.ds(i, 1), :]
            x_tile = xt[8 * tile:, :]
            red[i] = jnp.sum((feat * x_tile).reshape(length // 8, 8, rows), axis=0)
            return total + feat * row

        total = lax.fori_loop(0, 8, one, total, unroll=2)
        cross.append(total[:8])
        total = total[8:]
    cross_t = jnp.concatenate(cross, axis=0) + jnp.sum(red[...], axis=1)
    cross_q = (scale * np.sqrt(2.0)) * cross_t.T

    for copy in kv:
        copy.wait()
    keys = kk[...].reshape(2 * rows, width)
    vals = vv[...].reshape(2 * rows, width)

    def weights(q, g):
        score = dot(keys, q, NT)
        return scale * score * score, (2.0 * scale) * score * dot(vals, g, NT)

    attn, slope = weights(q_own, g_own)
    key_at = lax.broadcasted_iota(jnp.int32, (2 * rows, rows), 0)
    query_at = lax.broadcasted_iota(jnp.int32, (2 * rows, rows), 1) + core * rows
    causal = key_at <= query_at
    attn = jnp.where(causal, attn, 0.0).astype(jnp.bfloat16)
    slope = jnp.where(causal, slope, 0.0).astype(jnp.bfloat16)
    acc[:, :width] = dot(slope, q_own, NN)
    acc[:, width:] = dot(attn, g_own, NN)
    own_score = dot(q_own, kk[core], NT)
    own_slope = (2.0 * scale) * own_score * dot(g_own, vv[core], NT)
    own_causal = lax.broadcasted_iota(jnp.int32, (rows, rows), 1) <= lax.broadcasted_iota(
        jnp.int32, (rows, rows), 0
    )
    own_slope = jnp.where(own_causal, own_slope, 0.0).astype(jnp.bfloat16)
    dqb[0] = (dot(own_slope, kk[core], NN) + cross_q).astype(dqb.dtype)
    dq_out = pltpu.make_async_copy(dqb, dq_ref, out_sem.at[0])
    dq_out.start()

    def swap(dest, offset):
        return pltpu.make_async_remote_copy(
            src_ref=sb.at[dest],
            dst_ref=rb.at[offset],
            send_sem=x_send.at[offset],
            recv_sem=x_recv.at[offset],
            device_id={"query": dest % heads, "context": 2 * z + dest // heads},
            device_id_type=MESH,
        )

    def send_half(part):
        for dest in (0, heads):
            offset = lax.rem(dest - me + group, group)

            @pl.when(me != dest)
            def _():
                pltpu.make_async_remote_copy(
                    src_ref=sb.at[dest, :, part],
                    dst_ref=rb.at[offset, :, part],
                    send_sem=x_send.at[offset],
                    recv_sem=x_recv.at[offset],
                    device_id={"query": 0, "context": 2 * z + dest // heads},
                    device_id_type=MESH,
                ).start()

    def pack(part):
        sb[:, :, part] = acc[:, part].astype(jnp.bfloat16).reshape(group, share, width)

    key_half, value_half = pl.ds(0, width), pl.ds(width, width)

    batch, batches = later_batches(chips)

    def later(n, carry, last=False):
        first = 1 + n * batch
        for extra in range(batch):
            @pl.when(z + first + extra < chips)
            def _():
                for copy in down(first + extra):
                    copy.wait_recv()
        part = pl.ds(first, batch)
        q = qb[part].reshape(batch * rows, width)
        g = gb[part].reshape(batch * rows, width)
        attn, slope = weights(q, g)
        acc[:, width:] += dot(attn.astype(jnp.bfloat16), g, NN)
        if last:
            pack(value_half)
            send_half(value_half)
        acc[:, :width] += dot(slope.astype(jnp.bfloat16), q, NN)
        return carry

    if batches > 1:
        lax.fori_loop(0, batches - 1, later, 0)
    later(batches - 1, 0, True)

    pack(key_half)
    send_half(key_half)
    for head in range(1, heads):
        for half in range(2):
            dest = half * heads + head

            @pl.when(me != dest)
            def _():
                swap(dest, lax.rem(dest - me + group, group)).start()

    swaps = [swap(lax.rem(me + offset, group), offset) for offset in range(1, group)]
    mine = acc[pl.ds(pl.multiple_of(me * share, share), share), :]
    for offset, copy in enumerate(swaps, 1):
        copy.wait_recv()
        mine = mine + rb[offset].astype(jnp.float32)
    dkvb[0] = mine[:, :width].astype(dkvb.dtype)
    dkvb[1] = mine[:, width:].astype(dkvb.dtype)
    dkv_out = pltpu.make_async_copy(dkvb, dkv_ref, out_sem.at[1])
    dkv_out.start()

    for copy in swaps:
        copy.wait_send()
    for step in range(1, chips):
        @pl.when(z >= step)
        def _():
            for copy in down(step):
                copy.wait_send()
    dq_out.wait()
    dkv_out.wait()


def body(queries, keys, values, out_grad, prefix_states):
    heads = lax.axis_size("query")
    chips = lax.axis_size("context") // 2
    group = 2 * heads
    rows, width = keys.shape
    features = prefix_states.shape[1]
    share = rows // heads
    chunks = chunk_count(features)
    batch, batches = later_batches(chips)
    slots = 1 + batch * batches
    whole = jax.ShapeDtypeStruct(queries.shape, jnp.bfloat16)
    half = jax.ShapeDtypeStruct((1, share, width), jnp.bfloat16)
    dma = pltpu.SemaphoreType.DMA
    grad_q, grad_kv = pl.pallas_call(
        kernel,
        out_shape=(whole, jax.ShapeDtypeStruct((2, share, width), jnp.bfloat16)),
        in_specs=[pl.BlockSpec(memory_space=pl.ANY)] * 5,
        out_specs=[pl.BlockSpec(memory_space=pl.ANY)] * 2,
        scratch_shapes=[
            pltpu.VMEM(queries.shape, jnp.bfloat16),
            pltpu.VMEM((2, share, width), jnp.bfloat16),
            pltpu.VMEM((2, rows, width), jnp.bfloat16),
            pltpu.VMEM((2, rows, width), jnp.bfloat16),
            pltpu.VMEM((slots, rows, width), jnp.bfloat16),
            pltpu.VMEM((slots, rows, width), jnp.bfloat16),
            pltpu.VMEM((features, width), jnp.bfloat16),
            pltpu.VMEM((features, rows), jnp.float32),
            pltpu.VMEM((width, rows), jnp.float32),
            pltpu.VMEM((width, 8, rows), jnp.float32),
            pltpu.VMEM((2 * rows, 2 * width), jnp.float32),
            pltpu.VMEM((group, share, 2 * width), jnp.bfloat16),
            pltpu.VMEM((group, share, 2 * width), jnp.bfloat16),
            dma((2,)),
            dma((4,)),
            dma((chunks,)),
            dma((2,)),
            dma((2,)),
            dma((2, chips)),
            dma((2, chips)),
            dma((group,)),
            dma((group,)),
        ],
        compiler_params=pltpu.CompilerParams(
            collective_id=0, has_side_effects=True, vmem_limit_bytes=55168 * 1024
        ),
        cost_estimate=pl.CostEstimate(
            flops=2 * features * width * rows, bytes_accessed=2 * features * width, transcendentals=0
        ),
        name="power_backward",
    )(queries, keys, values, out_grad, prefix_states)
    return pl.pallas_call(
        place,
        out_shape=(whole, half, half),
        in_specs=[pl.BlockSpec(memory_space=pl.ANY)] * 2,
        out_specs=[pl.BlockSpec(memory_space=pl.ANY)] * 3,
        scratch_shapes=[dma((3,))],
        compiler_params=pltpu.CompilerParams(vmem_limit_bytes=55168 * 1024),
        name="place_results",
    )(grad_q, grad_kv)


def solution(mesh):
    return jax.shard_map(
        body,
        mesh=mesh,
        in_specs=(
            P("query", "context", None),
            P("context", None),
            P("context", None),
            P("query", "context", None),
            P("context", None, None),
        ),
        out_specs=(
            P("query", "context", None),
            P("context", "query", None),
            P("context", "query", None),
        ),
        check_vma=False,
    )
```
